32 devices in a mesh: dp: 8 (over y, x, core), tensor: 4 (over z).
Axes of the slice: x: 2, y: 2, z: 4, core: 2. Of those that a mesh axis runs over, the one named last changes fastest.
Arguments:
- gate_act: bfloat16 [256, 14336], P('dp', 'tensor'), may hold values from -6 to 6
- up_act: bfloat16 [256, 14336], P('dp', 'tensor'), may hold values from -6 to 6
- cotangent: bfloat16 [256, 4096], P(('dp', 'tensor')), may hold values from -6 to 6
- down_blocks: bfloat16 [112, 2048, 128], P('tensor'), may hold values from -0.125 to 0.125
- down_index: int32 [112, 16], P('tensor'), may hold values from 0 to 31, as said below
Outputs:
- down_grad: float32 [2048, 112, 128], P('dp', 'tensor')
- gate_grad: bfloat16 [256, 14336], P('dp', 'tensor')
- up_grad: bfloat16 [256, 14336], P('dp', 'tensor')
The draws below stay inside these ranges and needn't reach their ends.
Inputs may be any that keep to these rules, and one draw needn't show every extreme that they name: `down_index`: each row names 16 distinct feature blocks.
All inputs are finite; a program needn't handle non-finite values.
Results may differ from the reference program's by a relative error of at most 0.0029.
Values may be sent and summed in bfloat16 or wider, within the bound.
No kernel may reach another device: no remote copies, remote signals or barrier semaphores. Data moves between devices by JAX's collectives and lax.ppermute only.
A program may use at most 128 MiB of HBM per device.

```python
import jax
import jax.numpy as jnp
from jax import lax

D = 4096
FF = 14336
BS = 128
DB = 32
KEEP = 16
FFB = 112
TOKENS = 256
N_DP = 8


def draw_down_index(key, part):
    key = jax.random.fold_in(key, 5)
    scores = jax.random.randint(key, (FFB, DB), 0, 1048576) * DB + jnp.arange(DB, dtype=jnp.int32)[None, :]
    order = jnp.argsort(scores, axis=1, stable=True)
    return order[:, :KEEP].astype(jnp.int32)


def block_levels(own_key, extent, cuts, smallest, largest):
    level = 1.0
    for position, shards_of in cuts:
        draws = jax.random.uniform(jax.random.fold_in(jax.random.fold_in(own_key, 6), position), (shards_of,), jnp.float32, smallest / len(cuts), largest / len(cuts))
        level = level * jnp.repeat(jnp.exp(draws), extent[position] // shards_of).reshape((-1,) + (1,) * (len(extent) - 1 - position))
    return level


def normal_values(stream_key, extent, spread, bound, split=(), kind=jnp.bfloat16):
    values = spread * jax.random.normal(stream_key, extent, jnp.float32)
    if split:
        values = values * block_levels(stream_key, extent, split, -0.22, 0.18)
    return jnp.clip(values, -bound, bound).astype(kind)


def setup_inputs(seed: int = 0) -> dict:
    keys = jax.random.split(jax.random.key(seed), 6)
    gate_act = normal_values(keys[0], (TOKENS, FF), 1.0, 6.0, ((0, 8), (1, 4)))
    up_act = normal_values(keys[1], (TOKENS, FF), 1.0, 6.0, ((0, 8), (1, 4)))
    cotangent = normal_values(keys[2], (TOKENS, D), 1.0, 6.0, ((0, 32),))
    down_blocks = normal_values(keys[3], (FFB, KEEP * BS, BS), (KEEP * BS) ** -0.5, 0.125, ((0, 4),))
    down_index = draw_down_index(jax.random.fold_in(keys[5], 71), 0)
    return {"gate_act": gate_act, "up_act": up_act, "cotangent": cotangent, "down_blocks": down_blocks, "down_index": down_index}


def reference(gate_act, up_act, cotangent, down_blocks, down_index):
    token_count = cotangent.shape[0]
    gate_value = gate_act.astype(jnp.float32).reshape(token_count, FFB, BS).transpose(1, 0, 2)
    up_value = up_act.astype(jnp.float32).reshape(token_count, FFB, BS).transpose(1, 0, 2)
    feature_view = cotangent.reshape(token_count, DB, BS)

    def one_block(inputs):
        index_row, weight_block, gate_block, up_block = inputs
        chosen = jnp.take(feature_view, index_row.astype(jnp.int32), axis=1).reshape(token_count, KEEP * BS)
        sigmoid_gate = jax.nn.sigmoid(gate_block)
        hidden = (gate_block * sigmoid_gate * up_block).astype(jnp.bfloat16)
        hidden_grad = jnp.dot(chosen, weight_block, preferred_element_type=jnp.float32)
        gate_out = (hidden_grad * up_block * sigmoid_gate * (1.0 + gate_block * (1.0 - sigmoid_gate))).astype(jnp.bfloat16)
        up_out = (hidden_grad * gate_block * sigmoid_gate).astype(jnp.bfloat16)
        weight_grad = jnp.dot(chosen.T, hidden, preferred_element_type=jnp.float32)
        return weight_grad, gate_out, up_out

    weight_grad, gate_out, up_out = lax.map(one_block, (down_index, down_blocks, gate_value, up_value))
    down_grad = weight_grad.transpose(1, 0, 2) / N_DP
    gate_grad = gate_out.transpose(1, 0, 2).reshape(token_count, FF)
    up_grad = up_out.transpose(1, 0, 2).reshape(token_count, FF)
    return down_grad, gate_grad, up_grad
```

```python
import functools

import jax
import jax.numpy as jnp
from jax import lax
from jax.experimental import pallas as pl
from jax.experimental.pallas import tpu as pltpu
from jax.sharding import PartitionSpec as P


def reduced(gate_act, up_act, cotangent, down_blocks, down_index):
    gathered = lax.all_gather(cotangent, "tensor", axis=0, tiled=True)
    row_count = gathered.shape[0]
    local_blocks, kept_span, block_size = down_blocks.shape
    feature_count = gathered.shape[1] // block_size
    feature_view = gathered.reshape(row_count, feature_count, block_size)
    gate_value = gate_act.astype(jnp.float32).reshape(row_count, local_blocks, block_size)
    up_value = up_act.astype(jnp.float32).reshape(row_count, local_blocks, block_size)
    sigmoid_gate = jax.nn.sigmoid(gate_value)
    hidden = (gate_value * sigmoid_gate * up_value).astype(jnp.bfloat16)
    hidden_blocks = hidden.transpose(1, 0, 2)
    replicas = lax.axis_size("dp")

    def select(index_row):
        return jnp.take(feature_view, index_row, axis=1).reshape(row_count, kept_span)

    def one_grad(inputs):
        index_row, weight_block = inputs
        return jnp.dot(select(index_row), weight_block, preferred_element_type=jnp.float32)

    hidden_grad = lax.map(one_grad, (down_index, down_blocks)).transpose(1, 0, 2)
    gate_out = (
        (hidden_grad * up_value * sigmoid_gate * (1.0 + gate_value * (1.0 - sigmoid_gate)))
        .astype(jnp.bfloat16)
        .reshape(row_count, local_blocks * block_size)
    )
    up_out = (
        (hidden_grad * gate_value * sigmoid_gate)
        .astype(jnp.bfloat16)
        .reshape(row_count, local_blocks * block_size)
    )

    def one_term(inputs):
        index_row, hidden_block = inputs
        part_rows = select(index_row)
        return jnp.dot(part_rows.T, hidden_block, preferred_element_type=jnp.float32)

    summed = lax.psum_scatter(
        lax.map(one_term, (down_index, hidden_blocks)).transpose(1, 0, 2),
        "dp",
        scatter_dimension=0,
        tiled=True,
    )
    down_grad = summed / replicas
    return (down_grad, gate_out, up_out)


def hidden_grad_kernel(index_ref, cot_ref, weight_ref, gate_ref, up_ref, gate_out, up_out, *, per_step, keep):
    step = pl.program_id(0)
    for j in range(per_step):
        block = step * per_step + j
        chosen = jnp.concatenate(
            [cot_ref[:, pl.ds(pl.multiple_of(index_ref[block, k] * 128, 128), 128)] for k in range(keep)], axis=1
        )
        grad = jnp.dot(chosen, weight_ref[j], preferred_element_type=jnp.float32)
        span = slice(j * 128, (j + 1) * 128)
        gate = gate_ref[:, span].astype(jnp.float32)
        up = up_ref[:, span].astype(jnp.float32)
        sig = jax.nn.sigmoid(gate)
        gate_out[:, span] = (grad * up * sig * (1.0 + gate * (1.0 - sig))).astype(jnp.bfloat16)
        up_out[:, span] = (grad * gate * sig).astype(jnp.bfloat16)


def hidden_grads(index, cot, weights, gate, up, per_step=4):
    blocks, span, size = weights.shape
    rows = cot.shape[0]
    wide = pl.BlockSpec((rows, per_step * size), lambda f, *_: (0, f))
    return pl.pallas_call(
        functools.partial(hidden_grad_kernel, per_step=per_step, keep=span // size),
        grid_spec=pltpu.PrefetchScalarGridSpec(
            num_scalar_prefetch=1,
            grid=(blocks // per_step,),
            in_specs=[
                pl.BlockSpec(cot.shape, lambda f, *_: (0, 0)),
                pl.BlockSpec((per_step, span, size), lambda f, *_: (f, 0, 0)),
                wide,
                wide,
            ],
            out_specs=[wide, wide],
        ),
        out_shape=[jax.ShapeDtypeStruct(gate.shape, gate.dtype)] * 2,
        compiler_params=pltpu.CompilerParams(vmem_limit_bytes=32 * 2**20),
        cost_estimate=pl.CostEstimate(
            flops=2 * rows * blocks * span * size, bytes_accessed=2 * blocks * span * size, transcendentals=0
        ),
        name="hidden_grads",
    )(index, cot, weights, gate, up)


def down_grad_kernel(index_ref, *refs, pieces, per_step, kept, features, scale):
    hidden, cot, out_ref, turned = refs[:pieces], refs[pieces : 2 * pieces], refs[2 * pieces], refs[2 * pieces + 1]
    step = pl.program_id(0)

    @pl.when(step == 0)
    def _():
        for d in range(features):
            span = slice(d * 128, (d + 1) * 128)
            turned[d] = jnp.concatenate([c[:, span] for c in cot], axis=0).T

    for j in range(per_step):
        block = step * per_step + j
        right = jnp.concatenate([h[:, j * 128 : (j + 1) * 128] for h in hidden], axis=0)
        for k in range(kept):
            left = turned[index_ref[block, k]]
            out_ref[j, k * 128 : (k + 1) * 128, :] = jnp.dot(left, right, preferred_element_type=jnp.float32) * scale


def down_grads(index, hidden, cot, scale, per_step=4):
    rows, width = hidden[0].shape
    pieces = len(hidden)
    kept = index.shape[1]
    blocks = width // 128
    features = cot[0].shape[1] // 128
    tokens = pieces * rows
    return pl.pallas_call(
        functools.partial(
            down_grad_kernel, pieces=pieces, per_step=per_step, kept=kept, features=features, scale=scale
        ),
        grid_spec=pltpu.PrefetchScalarGridSpec(
            num_scalar_prefetch=1,
            grid=(blocks // per_step,),
            in_specs=[pl.BlockSpec((rows, per_step * 128), lambda f, *_: (0, f))] * pieces
            + [pl.BlockSpec(c.shape, lambda f, *_: (0, 0)) for c in cot],
            out_specs=pl.BlockSpec((per_step, kept * 128, 128), lambda f, *_: (f, 0, 0)),
            scratch_shapes=[pltpu.VMEM((features, 128, tokens), jnp.bfloat16)],
        ),
        out_shape=jax.ShapeDtypeStruct((blocks, kept * 128, 128), jnp.float32),
        compiler_params=pltpu.CompilerParams(vmem_limit_bytes=32 * 2**20),
        cost_estimate=pl.CostEstimate(
            flops=2 * tokens * kept * 128 * width, bytes_accessed=4 * blocks * kept * 128 * 128, transcendentals=0
        ),
        name="down_grads",
    )(index, *hidden, *cot)


def spread(own, size):
    first = [(i, i ^ (2 if i % 2 == 0 else 4)) for i in range(size)]
    second = [(i, i ^ (4 if i % 2 == 0 else 2)) for i in range(size)]
    other = [(i, i ^ 1) for i in range(size)]
    step = functools.partial(lax.ppermute, axis_name="dp")
    one = step(own, perm=first)
    two = step(own, perm=second)
    three = step(one, perm=second)
    mine = [own, one, two, three]
    return mine + [step(piece, perm=other) for piece in mine]


def gathered(gate_act, up_act, cotangent, down_blocks, down_index):
    replicas = lax.axis_size("dp")
    parts = lax.axis_size("tensor")
    rows, width = gate_act.shape
    kept = down_index.shape[1] // replicas

    gate_value = gate_act.astype(jnp.float32)
    hidden = (gate_value * jax.nn.sigmoid(gate_value) * up_act.astype(jnp.float32)).astype(jnp.bfloat16)

    cot = lax.all_gather(cotangent, "tensor", axis=0, tiled=True)
    hidden_pieces = spread(hidden, replicas)
    cot_pieces = spread(cot, replicas)
    gate_out, up_out = hidden_grads(down_index, cot, down_blocks, gate_act, up_act)
    own_index = lax.dynamic_slice_in_dim(down_index, lax.axis_index("dp") * kept, kept, axis=1)
    down_grad = down_grads(own_index, hidden_pieces, cot_pieces, 1.0 / replicas)
    return down_grad.transpose(1, 0, 2), gate_out, up_out


def local(gate_act, up_act, cotangent, down_blocks, down_index):
    if lax.axis_size("dp") == 8 and gate_act.shape[0] % 16 == 0 and gate_act.shape[0] <= 64:
        return gathered(gate_act, up_act, cotangent, down_blocks, down_index)
    return reduced(gate_act, up_act, cotangent, down_blocks, down_index)


def solution(mesh):
    in_specs = (
        P("dp", "tensor"),
        P("dp", "tensor"),
        P(("dp", "tensor"), None),
        P("tensor", None, None),
        P("tensor", None),
    )
    out_specs = (P("dp", "tensor", None), P("dp", "tensor"), P("dp", "tensor"))
    return jax.shard_map(local, mesh=mesh, in_specs=in_specs, out_specs=out_specs, check_vma=False)
```

```python
import functools

import jax
import jax.numpy as jnp
from jax import lax
from jax.experimental import pallas as pl
from jax.experimental.pallas import tpu as pltpu
from jax.sharding import PartitionSpec as P


def reduced(gate_act, up_act, cotangent, down_blocks, down_index):
    gathered = lax.all_gather(cotangent, "tensor", axis=0, tiled=True)
    row_count = gathered.shape[0]
    local_blocks, kept_span, block_size = down_blocks.shape
    feature_count = gathered.shape[1] // block_size
    feature_view = gathered.reshape(row_count, feature_count, block_size)
    gate_value = gate_act.astype(jnp.float32).reshape(row_count, local_blocks, block_size)
    up_value = up_act.astype(jnp.float32).reshape(row_count, local_blocks, block_size)
    sigmoid_gate = jax.nn.sigmoid(gate_value)
    hidden = (gate_value * sigmoid_gate * up_value).astype(jnp.bfloat16)
    hidden_blocks = hidden.transpose(1, 0, 2)
    replicas = lax.axis_size("dp")

    def select(index_row):
        return jnp.take(feature_view, index_row, axis=1).reshape(row_count, kept_span)

    def one_grad(inputs):
        index_row, weight_block = inputs
        return jnp.dot(select(index_row), weight_block, preferred_element_type=jnp.float32)

    hidden_grad = lax.map(one_grad, (down_index, down_blocks)).transpose(1, 0, 2)
    gate_out = (
        (hidden_grad * up_value * sigmoid_gate * (1.0 + gate_value * (1.0 - sigmoid_gate)))
        .astype(jnp.bfloat16)
        .reshape(row_count, local_blocks * block_size)
    )
    up_out = (
        (hidden_grad * gate_value * sigmoid_gate)
        .astype(jnp.bfloat16)
        .reshape(row_count, local_blocks * block_size)
    )

    def one_term(inputs):
        index_row, hidden_block = inputs
        part_rows = select(index_row)
        return jnp.dot(part_rows.T, hidden_block, preferred_element_type=jnp.float32)

    summed = lax.psum_scatter(
        lax.map(one_term, (down_index, hidden_blocks)).transpose(1, 0, 2),
        "dp",
        scatter_dimension=0,
        tiled=True,
    )
    down_grad = summed / replicas
    return (down_grad, gate_out, up_out)


IN_VMEM = pl.BlockSpec(memory_space=pltpu.VMEM)
IN_SMEM = pl.BlockSpec(memory_space=pltpu.SMEM)
ANYWHERE = pl.BlockSpec(memory_space=pl.ANY)


def resident(array):
    return pltpu.with_memory_space_constraint(array, pltpu.VMEM)


def remaining(array):
    return pltpu.with_memory_space_constraint(array, pltpu.HBM)


def assemble_kernel(*refs, parts):
    pieces, out_ref = refs[:parts], refs[-1]
    here = lax.axis_index("tensor")
    for place in range(parts):

        @pl.when(here == place)
        def _():
            out_ref[...] = jnp.concatenate([pieces[place ^ q][...] for q in range(parts)], axis=0)


def assemble(pieces, after):
    rows, width = pieces[0].shape
    parts = len(pieces)
    return pl.pallas_call(
        functools.partial(assemble_kernel, parts=parts),
        in_specs=[IN_VMEM] * (parts + len(after)),
        out_specs=IN_VMEM,
        out_shape=pltpu.VMEM((parts * rows, width), pieces[0].dtype),
        compiler_params=pltpu.CompilerParams(vmem_limit_bytes=4 * 2**20),
        name="assemble",
    )(*map(resident, pieces), *map(resident, after))


def hidden_kernel(*refs, kept):
    sources, hidden_ref, targets, sems = refs[:kept], refs[kept], refs[kept + 1 : -1], refs[-1]
    loads = [pltpu.make_async_copy(source, target, sems.at[i]) for i, (source, target) in enumerate(zip(sources, targets))]
    for load in loads:
        load.start()
    for load in loads:
        load.wait()
    gate = targets[0][...].astype(jnp.float32)
    up = targets[1][...].astype(jnp.float32)
    hidden_ref[...] = (gate * jax.nn.sigmoid(gate) * up).astype(hidden_ref.dtype)


def hidden_units(*arrays):
    outs = [pltpu.VMEM(array.shape, array.dtype) for array in arrays]
    return pl.pallas_call(
        functools.partial(hidden_kernel, kept=len(arrays)),
        in_specs=[ANYWHERE] * len(arrays),
        out_specs=[IN_VMEM] * (1 + len(arrays)),
        out_shape=[outs[0]] + outs,
        scratch_shapes=[pltpu.SemaphoreType.DMA((len(arrays),))],
        compiler_params=pltpu.CompilerParams(vmem_limit_bytes=4 * 2**20),
        name="hidden_units",
    )(*map(remaining, arrays))


def fetch_kernel(weight_ref, out_ref, sems, *, start, chunk):
    blocks = out_ref.shape[0]
    loads = [
        pltpu.make_async_copy(weight_ref.at[pl.ds(start + j, chunk)], out_ref.at[pl.ds(j, chunk)], sems.at[j // chunk])
        for j in range(0, blocks, chunk)
    ]
    for load in loads:
        load.start()
    for load in loads:
        load.wait()


def fetch(weights, start, blocks, chunk=2):
    return pl.pallas_call(
        functools.partial(fetch_kernel, start=start, chunk=chunk),
        in_specs=[ANYWHERE],
        out_specs=IN_VMEM,
        out_shape=pltpu.VMEM((blocks,) + weights.shape[1:], weights.dtype),
        scratch_shapes=[pltpu.SemaphoreType.DMA((blocks // chunk,))],
        compiler_params=pltpu.CompilerParams(vmem_limit_bytes=4 * 2**20),
        cost_estimate=pl.CostEstimate(flops=0, bytes_accessed=2**25, transcendentals=0),
        name="fetch",
    )(remaining(weights))


def hidden_grad_kernel(index_ref, cot_ref, gate_ref, up_ref, held, weight_ref, gate_out, up_out, rest, sems, *, chunk):
    ready, span, size = held.shape
    loads = [
        pltpu.make_async_copy(weight_ref.at[pl.ds(ready + j, chunk)], rest.at[pl.ds(j, chunk)], sems.at[j // chunk])
        for j in range(0, rest.shape[0], chunk)
    ]
    for load in loads:
        load.start()
    for block in range(weight_ref.shape[0]):
        chosen = jnp.concatenate(
            [cot_ref[:, pl.ds(pl.multiple_of(index_ref[k, block] * size, size), size)] for k in range(span // size)],
            axis=1,
        )
        if block < ready:
            weight = held[block]
        else:
            if (block - ready) % chunk == 0:
                loads[(block - ready) // chunk].wait()
            weight = rest[block - ready]
        grad = jnp.dot(chosen, weight, preferred_element_type=jnp.float32)
        here = slice(block * size, (block + 1) * size)
        gate = gate_ref[:, here].astype(jnp.float32)
        up = up_ref[:, here].astype(jnp.float32)
        sig = jax.nn.sigmoid(gate)
        gate_out[:, here] = (grad * up * sig * (1.0 + gate * (1.0 - sig))).astype(jnp.bfloat16)
        up_out[:, here] = (grad * gate * sig).astype(jnp.bfloat16)


def hidden_grads(index, cot, gate, up, held, weights, chunk=2):
    blocks, span, size = weights.shape
    rows = cot.shape[0]
    left = blocks - held.shape[0]
    return pl.pallas_call(
        functools.partial(hidden_grad_kernel, chunk=chunk),
        in_specs=[IN_SMEM] + [IN_VMEM] * 4 + [ANYWHERE],
        out_specs=[IN_VMEM] * 2,
        out_shape=[jax.ShapeDtypeStruct(gate.shape, gate.dtype)] * 2,
        scratch_shapes=[
            pltpu.VMEM((left, span, size), weights.dtype),
            pltpu.SemaphoreType.DMA((left // chunk,)),
        ],
        compiler_params=pltpu.CompilerParams(vmem_limit_bytes=10 * 2**20),
        cost_estimate=pl.CostEstimate(
            flops=2 * rows * blocks * span * size, bytes_accessed=2 * blocks * span * size, transcendentals=0
        ),
        name="hidden_grads",
    )(index, *map(resident, (cot, gate, up, held)), remaining(weights))


def turn_kernel(*refs):
    pieces, out_ref = refs[:-1], refs[-1]
    for d in range(out_ref.shape[0]):
        span = slice(d * 128, (d + 1) * 128)
        out_ref[d] = jnp.concatenate([piece[:, span] for piece in pieces], axis=0).T


def turn(pieces):
    rows, width = pieces[0].shape
    return pl.pallas_call(
        turn_kernel,
        in_specs=[IN_VMEM] * len(pieces),
        out_specs=IN_VMEM,
        out_shape=pltpu.VMEM((width // 128, 128, len(pieces) * rows), pieces[0].dtype),
        compiler_params=pltpu.CompilerParams(vmem_limit_bytes=4 * 2**20),
        name="turn",
    )(*map(resident, pieces))


def down_grad_kernel(index_ref, *refs, halves, pieces, kept, chunk, scale):
    turned, hidden = refs[:halves], refs[halves : halves + pieces]
    out_ref, held, sems = refs[halves + pieces :]
    first = lax.axis_index("dp") * kept
    blocks = held.shape[0]
    copies = []
    for start in range(0, blocks, chunk):
        for block in range(start, start + chunk):
            right = jnp.concatenate([h[:, block * 128 : (block + 1) * 128] for h in hidden], axis=0)
            left = jnp.concatenate(
                [jnp.concatenate([t[index_ref[first + k, block]] for t in turned], axis=1) for k in range(kept)], axis=0
            )
            held[block] = jnp.dot(left, right, preferred_element_type=jnp.float32) * scale
        span = pl.ds(start, chunk)
        copy = pltpu.make_async_copy(held.at[span], out_ref.at[span], sems.at[start // chunk])
        copy.start()
        copies.append(copy)
    for copy in copies:
        copy.wait()


def down_grads(index, turned, hidden, kept, scale, chunk=4):
    rows, width = hidden[0].shape
    pieces = len(hidden)
    blocks = width // 128
    shape = (blocks, kept * 128, 128)
    return pl.pallas_call(
        functools.partial(
            down_grad_kernel, halves=len(turned), pieces=pieces, kept=kept, chunk=chunk, scale=scale
        ),
        in_specs=[IN_SMEM] + [IN_VMEM] * (len(turned) + pieces),
        out_specs=ANYWHERE,
        out_shape=jax.ShapeDtypeStruct(shape, jnp.float32),
        scratch_shapes=[pltpu.VMEM(shape, jnp.float32), pltpu.SemaphoreType.DMA((blocks // chunk,))],
        compiler_params=pltpu.CompilerParams(vmem_limit_bytes=12 * 2**20),
        cost_estimate=pl.CostEstimate(
            flops=2 * pieces * rows * kept * 128 * width, bytes_accessed=4 * kept * 128 * width, transcendentals=0
        ),
        name="down_grads",
    )(index, *map(resident, turned), *map(resident, hidden))


def gathered(gate_act, up_act, cotangent, down_blocks, down_index):
    replicas = lax.axis_size("dp")
    parts = lax.axis_size("tensor")
    kept = down_index.shape[1] // replicas

    first = functools.partial(
        lax.ppermute, axis_name="dp", perm=[(i, i ^ (2 if i % 2 == 0 else 4)) for i in range(replicas)]
    )
    second = functools.partial(
        lax.ppermute, axis_name="dp", perm=[(i, i ^ (4 if i % 2 == 0 else 2)) for i in range(replicas)]
    )
    other = functools.partial(lax.ppermute, axis_name="dp", perm=[(i, i ^ 1) for i in range(replicas)])

    hidden, gate, up, index, near = hidden_units(gate_act, up_act, down_index.T, cotangent)
    h1, h2, h0x = first(hidden), second(hidden), other(hidden)
    slices = [near] + [
        lax.ppermute(cotangent, "tensor", [(i, i ^ s) for i in range(parts)]) for s in range(1, parts)
    ]
    held = fetch(down_blocks, 0, 20)
    cot = assemble(slices, [h1, h2, held])
    h3 = second(h1)
    c1, c2, c0x = first(cot), second(cot), other(cot)
    h1x, h2x = other(h1), other(h2)
    grads = hidden_grads(index, cot, gate, up, held, down_blocks)
    c1, c2, grads, h3 = lax.optimization_barrier((c1, c2, grads, h3))
    gate_out, up_out = grads
    c3 = second(c1)
    c1x, c2x, h3x = other(c1), other(c2), other(h3)
    early = turn([cot, c0x, c1, c1x])
    c3, early, h0x, h1x, h2x, h3x, c2x = lax.optimization_barrier((c3, early, h0x, h1x, h2x, h3x, c2x))
    c3x = other(c3)
    late = turn([c2, c2x, c3, c3x])
    pieces = [hidden, h0x, h1, h1x, h2, h2x, h3, h3x]
    down_grad = down_grads(index, [early, late], pieces, kept, 1.0 / replicas)
    return down_grad.transpose(1, 0, 2), gate_out, up_out


def local(gate_act, up_act, cotangent, down_blocks, down_index):
    sizes = (lax.axis_size("dp"), lax.axis_size("tensor"), gate_act.shape[0], down_blocks.shape[0] % 4)
    if sizes == (8, 4, 32, 0):
        return gathered(gate_act, up_act, cotangent, down_blocks, down_index)
    return reduced(gate_act, up_act, cotangent, down_blocks, down_index)


def solution(mesh):
    in_specs = (
        P("dp", "tensor"),
        P("dp", "tensor"),
        P(("dp", "tensor"), None),
        P("tensor", None, None),
        P("tensor", None),
    )
    out_specs = (P("dp", "tensor", None), P("dp", "tensor"), P("dp", "tensor"))
    return jax.shard_map(local, mesh=mesh, in_specs=in_specs, out_specs=out_specs, check_vma=False)
```

```python
import functools

import jax
import jax.numpy as jnp
from jax import lax
from jax.experimental import pallas as pl
from jax.experimental.pallas import tpu as pltpu
from jax.sharding import PartitionSpec as P


def reduced(gate_act, up_act, cotangent, down_blocks, down_index):
    gathered = lax.all_gather(cotangent, "tensor", axis=0, tiled=True)
    row_count = gathered.shape[0]
    local_blocks, kept_span, block_size = down_blocks.shape
    feature_count = gathered.shape[1] // block_size
    feature_view = gathered.reshape(row_count, feature_count, block_size)
    gate_value = gate_act.astype(jnp.float32).reshape(row_count, local_blocks, block_size)
    up_value = up_act.astype(jnp.float32).reshape(row_count, local_blocks, block_size)
    sigmoid_gate = jax.nn.sigmoid(gate_value)
    hidden = (gate_value * sigmoid_gate * up_value).astype(jnp.bfloat16)
    hidden_blocks = hidden.transpose(1, 0, 2)
    replicas = lax.axis_size("dp")

    def select(index_row):
        return jnp.take(feature_view, index_row, axis=1).reshape(row_count, kept_span)

    def one_grad(inputs):
        index_row, weight_block = inputs
        return jnp.dot(select(index_row), weight_block, preferred_element_type=jnp.float32)

    hidden_grad = lax.map(one_grad, (down_index, down_blocks)).transpose(1, 0, 2)
    gate_out = (
        (hidden_grad * up_value * sigmoid_gate * (1.0 + gate_value * (1.0 - sigmoid_gate)))
        .astype(jnp.bfloat16)
        .reshape(row_count, local_blocks * block_size)
    )
    up_out = (
        (hidden_grad * gate_value * sigmoid_gate)
        .astype(jnp.bfloat16)
        .reshape(row_count, local_blocks * block_size)
    )

    def one_term(inputs):
        index_row, hidden_block = inputs
        part_rows = select(index_row)
        return jnp.dot(part_rows.T, hidden_block, preferred_element_type=jnp.float32)

    summed = lax.psum_scatter(
        lax.map(one_term, (down_index, hidden_blocks)).transpose(1, 0, 2),
        "dp",
        scatter_dimension=0,
        tiled=True,
    )
    down_grad = summed / replicas
    return (down_grad, gate_out, up_out)


LONG = 2**27
IN_VMEM = pl.BlockSpec(memory_space=pltpu.VMEM)
IN_SMEM = pl.BlockSpec(memory_space=pltpu.SMEM)
ANYWHERE = pl.BlockSpec(memory_space=pl.ANY)


def resident(array):
    return pltpu.with_memory_space_constraint(array, pltpu.VMEM)


def remaining(array):
    return pltpu.with_memory_space_constraint(array, pltpu.HBM)


def assemble_kernel(*refs, parts):
    pieces, out_ref = refs[:parts][::-1], refs[-1]
    here = lax.axis_index("tensor")
    for place in range(parts):

        @pl.when(here == place)
        def _():
            out_ref[...] = jnp.concatenate([pieces[place ^ q][...] for q in range(parts)], axis=0)


def assemble(pieces, after):
    rows, width = pieces[0].shape
    parts = len(pieces)
    return pl.pallas_call(
        functools.partial(assemble_kernel, parts=parts),
        in_specs=[IN_VMEM] * (parts + len(after)),
        out_specs=IN_VMEM,
        out_shape=pltpu.VMEM((parts * rows, width), pieces[0].dtype),
        compiler_params=pltpu.CompilerParams(vmem_limit_bytes=4 * 2**20),
        cost_estimate=pl.CostEstimate(flops=0, bytes_accessed=LONG, transcendentals=0),
        name="assemble",
    )(*map(resident, pieces[::-1]), *map(resident, after))


def hidden_kernel(*refs, kept):
    sources, hidden_ref, targets, sems = refs[:kept], refs[kept], refs[kept + 1 : -1], refs[-1]
    loads = [pltpu.make_async_copy(source, target, sems.at[i]) for i, (source, target) in enumerate(zip(sources, targets))]
    for load in loads:
        load.start()
    for load in loads:
        load.wait()
    gate = targets[0][...].astype(jnp.float32)
    up = targets[1][...].astype(jnp.float32)
    hidden_ref[...] = (gate * jax.nn.sigmoid(gate) * up).astype(hidden_ref.dtype)


def hidden_units(*arrays):
    outs = [pltpu.VMEM(array.shape, array.dtype) for array in arrays]
    return pl.pallas_call(
        functools.partial(hidden_kernel, kept=len(arrays)),
        in_specs=[ANYWHERE] * len(arrays),
        out_specs=[IN_VMEM] * (1 + len(arrays)),
        out_shape=[outs[0]] + outs,
        scratch_shapes=[pltpu.SemaphoreType.DMA((len(arrays),))],
        compiler_params=pltpu.CompilerParams(vmem_limit_bytes=4 * 2**20),
        cost_estimate=pl.CostEstimate(flops=0, bytes_accessed=LONG, transcendentals=0),
        name="hidden_units",
    )(*map(remaining, arrays))


def fetch_kernel(weight_ref, *refs, start, chunk):
    out_ref, sems = refs[-2:]
    loads = [
        pltpu.make_async_copy(weight_ref.at[pl.ds(start + j, chunk)], out_ref.at[pl.ds(j, chunk)], sems.at[j // chunk])
        for j in range(0, out_ref.shape[0], chunk)
    ]
    for load in loads:
        load.start()
    for load in loads:
        load.wait()


def fetch(weights, start, blocks, after=(), chunk=2):
    shape = (blocks,) + weights.shape[1:]
    return pl.pallas_call(
        functools.partial(fetch_kernel, start=start, chunk=chunk),
        in_specs=[ANYWHERE] + [IN_VMEM] * len(after),
        out_specs=IN_VMEM,
        out_shape=pltpu.VMEM(shape, weights.dtype),
        scratch_shapes=[pltpu.SemaphoreType.DMA((blocks // chunk,))],
        compiler_params=pltpu.CompilerParams(vmem_limit_bytes=4 * 2**20),
        cost_estimate=pl.CostEstimate(flops=0, bytes_accessed=2**18 * blocks, transcendentals=0),
        name="fetch",
    )(remaining(weights), *map(resident, after))


def hidden_grad_kernel(*refs, start, fetched, earlier, ahead):
    index_ref, cot_ref, gate_ref, up_ref = refs[:4]
    held = refs[4 : 4 + fetched]
    done = refs[4 + fetched : 4 + fetched + earlier]
    span, size = held[0].shape[1:]
    if ahead:
        weight_ref, (gate_out, up_out, next_ref, sem) = refs[4 + fetched + earlier], refs[-4:]
        load = pltpu.make_async_copy(weight_ref.at[pl.ds(weight_ref.shape[0] - ahead, ahead)], next_ref, sem)
        load.start()
    else:
        gate_out, up_out = refs[-2:]
    places = [(ref, j) for ref in held for j in range(ref.shape[0])]
    for source, target in zip(done, (gate_out, up_out)):
        target[:, : start * size] = source[...]
    for block in range(start, gate_out.shape[1] // size):
        chosen = jnp.concatenate(
            [cot_ref[:, pl.ds(pl.multiple_of(index_ref[k, block] * size, size), size)] for k in range(span // size)],
            axis=1,
        )
        ref, j = places[block]
        grad = jnp.dot(chosen, ref[j], preferred_element_type=jnp.float32)
        here = slice(block * size, (block + 1) * size)
        gate = gate_ref[:, here].astype(jnp.float32)
        up = up_ref[:, here].astype(jnp.float32)
        sig = jax.nn.sigmoid(gate)
        gate_out[:, here] = (grad * up * sig * (1.0 + gate * (1.0 - sig))).astype(jnp.bfloat16)
        up_out[:, here] = (grad * gate * sig).astype(jnp.bfloat16)
    if ahead:
        load.wait()


def hidden_grads(index, cot, gate, up, held, start, stop, earlier=(), weights=None, ahead=0):
    _, span, size = held[0].shape
    rows = cot.shape[0]
    shape = (rows, stop * size)
    outs = [jax.ShapeDtypeStruct(shape, gate.dtype)] * 2
    if ahead:
        outs = [pltpu.VMEM(shape, gate.dtype)] * 2 + [pltpu.VMEM((ahead, span, size), weights.dtype)]
    return pl.pallas_call(
        functools.partial(
            hidden_grad_kernel, start=start, fetched=len(held), earlier=len(earlier), ahead=ahead
        ),
        in_specs=[IN_SMEM] + [IN_VMEM] * (3 + len(held) + len(earlier)) + [ANYWHERE] * bool(ahead),
        out_specs=[IN_VMEM] * len(outs),
        out_shape=outs,
        scratch_shapes=[pltpu.SemaphoreType.DMA] * bool(ahead),
        compiler_params=pltpu.CompilerParams(vmem_limit_bytes=4 * 2**20),
        cost_estimate=pl.CostEstimate(
            flops=2 * rows * (stop - start) * span * size,
            bytes_accessed=2 * (stop - start) * span * size,
            transcendentals=0,
        ),
        name="hidden_grads",
    )(
        index,
        *map(resident, (cot, gate, up, *held, *earlier)),
        *([remaining(weights)] if ahead else []),
    )


def pack_kernel(*refs, count):
    pieces, out_ref = refs[:count], refs[-1]
    rows = pieces[0].shape[0]
    for i, piece in enumerate(pieces):
        out_ref[i * rows : (i + 1) * rows, :] = piece[...]


def pack(pieces, after):
    rows, width = pieces[0].shape
    return pl.pallas_call(
        functools.partial(pack_kernel, count=len(pieces)),
        in_specs=[IN_VMEM] * (len(pieces) + len(after)),
        out_specs=IN_VMEM,
        out_shape=pltpu.VMEM((len(pieces) * rows, width), pieces[0].dtype),
        compiler_params=pltpu.CompilerParams(vmem_limit_bytes=4 * 2**20),
        cost_estimate=pl.CostEstimate(flops=0, bytes_accessed=LONG, transcendentals=0),
        name="pack",
    )(*map(resident, pieces), *map(resident, after))


def turn_kernel(*refs):
    pieces, out_ref = refs[:-1], refs[-1]
    for d in range(out_ref.shape[0]):
        span = slice(d * 128, (d + 1) * 128)
        out_ref[d] = jnp.concatenate([piece[:, span] for piece in pieces], axis=0).T


def turn(pieces):
    rows, width = pieces[0].shape
    return pl.pallas_call(
        turn_kernel,
        in_specs=[IN_VMEM] * len(pieces),
        out_specs=IN_VMEM,
        out_shape=pltpu.VMEM((width // 128, 128, len(pieces) * rows), pieces[0].dtype),
        compiler_params=pltpu.CompilerParams(vmem_limit_bytes=4 * 2**20),
        name="turn",
    )(*map(resident, pieces))


def down_grad_kernel(index_ref, *refs, halves, groups, rows, kept, chunk, scale):
    turned, hidden, (out_ref, held, sems) = refs[:halves], list(refs[halves:-3]), refs[-3:]
    pieces = []
    for count in groups:
        group = [hidden.pop(0) for _ in range(count)]
        pieces += [(h, i) for i in range(group[0].shape[0] // rows) for h in group]
    first = lax.axis_index("dp") * kept
    blocks = held.shape[0]
    copies = []
    for start in range(0, blocks, chunk):
        for block in range(start, start + chunk):
            span = slice(block * 128, (block + 1) * 128)
            right = jnp.concatenate([h[i * rows : (i + 1) * rows, span] for h, i in pieces], axis=0)
            left = jnp.concatenate(
                [jnp.concatenate([t[index_ref[first + k, block]] for t in turned], axis=1) for k in range(kept)], axis=0
            )
            held[block] = jnp.dot(left, right, preferred_element_type=jnp.float32) * scale
        span = pl.ds(start, chunk)
        copy = pltpu.make_async_copy(held.at[span], out_ref.at[span], sems.at[start // chunk])
        copy.start()
        copies.append(copy)
    for copy in copies:
        copy.wait()


def down_grads(index, turned, hidden, rows, kept, scale, chunk=4):
    width = hidden[0][0].shape[1]
    arrays = [array for group in hidden for array in group]
    tokens = sum(array.shape[0] for array in arrays)
    blocks = width // 128
    shape = (blocks, kept * 128, 128)
    return pl.pallas_call(
        functools.partial(
            down_grad_kernel, halves=len(turned), groups=list(map(len, hidden)), rows=rows, kept=kept, chunk=chunk, scale=scale
        ),
        in_specs=[IN_SMEM] + [IN_VMEM] * (len(turned) + len(arrays)),
        out_specs=ANYWHERE,
        out_shape=jax.ShapeDtypeStruct(shape, jnp.float32),
        scratch_shapes=[pltpu.VMEM(shape, jnp.float32), pltpu.SemaphoreType.DMA((blocks // chunk,))],
        compiler_params=pltpu.CompilerParams(vmem_limit_bytes=12 * 2**20),
        cost_estimate=pl.CostEstimate(
            flops=2 * tokens * kept * 128 * width, bytes_accessed=4 * kept * 128 * width, transcendentals=0
        ),
        name="down_grads",
    )(index, *map(resident, (*turned, *arrays)))


def gathered(gate_act, up_act, cotangent, down_blocks, down_index):
    replicas = lax.axis_size("dp")
    parts = lax.axis_size("tensor")
    kept = down_index.shape[1] // replicas

    first = functools.partial(
        lax.ppermute, axis_name="dp", perm=[(i, i ^ (2 if i % 2 == 0 else 4)) for i in range(replicas)]
    )
    second = functools.partial(
        lax.ppermute, axis_name="dp", perm=[(i, i ^ (4 if i % 2 == 0 else 2)) for i in range(replicas)]
    )
    across = functools.partial(lax.ppermute, axis_name="dp", perm=[(i, i ^ 6) for i in range(replicas)])
    other = functools.partial(lax.ppermute, axis_name="dp", perm=[(i, i ^ 1) for i in range(replicas)])

    slices = [lax.ppermute(cotangent, "tensor", [(i, i ^ s) for i in range(parts)]) for s in range(1, parts)]
    hidden, gate, up, index, near = hidden_units(gate_act, up_act, down_index.T, cotangent)
    h1, h2 = first(hidden), second(hidden)
    blocks = down_blocks.shape[0]
    half = blocks // 2
    ahead = blocks * 3 // 14
    held = [fetch(down_blocks, 0, blocks - ahead)]
    cot = assemble([near] + slices, [hidden, *held])
    c1, c2 = first(cot), second(cot)
    packed = pack([hidden, h1, h2], [cot])
    h3 = second(h1)
    packed_x, c0x = other(packed), other(cot)
    *grads, rest = hidden_grads(index, cot, gate, up, held, 0, half, weights=down_blocks, ahead=ahead)
    c1, c2, grads = lax.optimization_barrier((c1, c2, grads))
    c3 = second(c1)
    c1x, c2x = other(c1), other(c2)
    rest, h3 = lax.optimization_barrier((rest, h3))
    h3x = other(h3)
    grads = hidden_grads(index, cot, gate, up, held + [rest], half, blocks, grads)
    early = turn([cot, c0x, c1, c1x])
    c3, early, c2x, h3x, packed_x, (gate_out, up_out) = lax.optimization_barrier(
        (c3, early, c2x, h3x, packed_x, grads)
    )
    c3x = other(c3)
    late = turn([c2, c2x, c3, c3x])
    down_grad = down_grads(index, [early, late], [[packed, packed_x], [h3, h3x]], hidden.shape[0], kept, 1.0 / replicas)
    return down_grad.transpose(1, 0, 2), gate_out, up_out


def local(gate_act, up_act, cotangent, down_blocks, down_index):
    sizes = (lax.axis_size("dp"), lax.axis_size("tensor"), gate_act.shape[0], down_blocks.shape[0] % 4)
    if sizes == (8, 4, 32, 0):
        return gathered(gate_act, up_act, cotangent, down_blocks, down_index)
    return reduced(gate_act, up_act, cotangent, down_blocks, down_index)


def solution(mesh):
    in_specs = (
        P("dp", "tensor"),
        P("dp", "tensor"),
        P(("dp", "tensor"), None),
        P("tensor", None, None),
        P("tensor", None),
    )
    out_specs = (P("dp", "tensor", None), P("dp", "tensor"), P("dp", "tensor"))
    return jax.shard_map(local, mesh=mesh, in_specs=in_specs, out_specs=out_specs, check_vma=False)
```

```python
import functools

import jax
import jax.numpy as jnp
from jax import lax
from jax.experimental import pallas as pl
from jax.experimental.pallas import tpu as pltpu
from jax.sharding import PartitionSpec as P


def reduced(gate_act, up_act, cotangent, down_blocks, down_index):
    gathered = lax.all_gather(cotangent, "tensor", axis=0, tiled=True)
    row_count = gathered.shape[0]
    local_blocks, kept_span, block_size = down_blocks.shape
    feature_count = gathered.shape[1] // block_size
    feature_view = gathered.reshape(row_count, feature_count, block_size)
    gate_value = gate_act.astype(jnp.float32).reshape(row_count, local_blocks, block_size)
    up_value = up_act.astype(jnp.float32).reshape(row_count, local_blocks, block_size)
    sigmoid_gate = jax.nn.sigmoid(gate_value)
    hidden = (gate_value * sigmoid_gate * up_value).astype(jnp.bfloat16)
    hidden_blocks = hidden.transpose(1, 0, 2)
    replicas = lax.axis_size("dp")

    def select(index_row):
        return jnp.take(feature_view, index_row, axis=1).reshape(row_count, kept_span)

    def one_grad(inputs):
        index_row, weight_block = inputs
        return jnp.dot(select(index_row), weight_block, preferred_element_type=jnp.float32)

    hidden_grad = lax.map(one_grad, (down_index, down_blocks)).transpose(1, 0, 2)
    gate_out = (
        (hidden_grad * up_value * sigmoid_gate * (1.0 + gate_value * (1.0 - sigmoid_gate)))
        .astype(jnp.bfloat16)
        .reshape(row_count, local_blocks * block_size)
    )
    up_out = (
        (hidden_grad * gate_value * sigmoid_gate)
        .astype(jnp.bfloat16)
        .reshape(row_count, local_blocks * block_size)
    )

    def one_term(inputs):
        index_row, hidden_block = inputs
        part_rows = select(index_row)
        return jnp.dot(part_rows.T, hidden_block, preferred_element_type=jnp.float32)

    summed = lax.psum_scatter(
        lax.map(one_term, (down_index, hidden_blocks)).transpose(1, 0, 2),
        "dp",
        scatter_dimension=0,
        tiled=True,
    )
    down_grad = summed / replicas
    return (down_grad, gate_out, up_out)


LONG = 2**27
IN_VMEM = pl.BlockSpec(memory_space=pltpu.VMEM)
IN_SMEM = pl.BlockSpec(memory_space=pltpu.SMEM)
ANYWHERE = pl.BlockSpec(memory_space=pl.ANY)


def resident(array):
    return pltpu.with_memory_space_constraint(array, pltpu.VMEM)


def scalar(array):
    return pltpu.with_memory_space_constraint(array, pltpu.SMEM)


def remaining(array):
    return pltpu.with_memory_space_constraint(array, pltpu.HBM)


def assemble_kernel(*refs, parts):
    pieces, (out_ref, sent_ref) = refs[:parts][::-1], refs[-2:]
    here = lax.axis_index("tensor")
    for place in range(parts):

        @pl.when(here == place)
        def _():
            out_ref[...] = jnp.concatenate([pieces[place ^ q][...] for q in range(parts)], axis=0)

    width = out_ref.shape[1]
    sent_ref[:, :width] = jnp.concatenate([piece[...] for piece in pieces[2:]], axis=0)
    sent_ref[:, width:] = stacked(pieces[1][...])


def stacked(rows):
    half = rows.shape[1] // 2
    return jnp.concatenate([rows[:, :half], rows[:, half:]], axis=0)


def assemble(pieces, after):
    rows, width = pieces[0].shape
    parts = len(pieces)
    dtype = pieces[0].dtype
    return pl.pallas_call(
        functools.partial(assemble_kernel, parts=parts),
        in_specs=[IN_VMEM] * (parts + len(after)),
        out_specs=[IN_VMEM] * 2,
        out_shape=[pltpu.VMEM((parts * rows, width), dtype), pltpu.VMEM((2 * rows, width * 3 // 2), dtype)],
        compiler_params=pltpu.CompilerParams(vmem_limit_bytes=4 * 2**20),
        cost_estimate=pl.CostEstimate(flops=0, bytes_accessed=LONG, transcendentals=0),
        name="assemble",
    )(*map(resident, pieces[::-1]), *map(resident, after))


def hidden_kernel(*refs, kept):
    sources, message_ref, targets, (hidden, sems) = refs[:kept], refs[kept], refs[kept + 1 : -2], refs[-2:]
    loads = [pltpu.make_async_copy(source, target, sems.at[i]) for i, (source, target) in enumerate(zip(sources, targets))]
    for load in loads:
        load.start()
    for load in loads:
        load.wait()
    gate = targets[0][...].astype(jnp.float32)
    up = targets[1][...].astype(jnp.float32)
    hidden[...] = gate * jax.nn.sigmoid(gate) * up
    rows, width = hidden.shape
    cot = targets[-1]
    size = cot.shape[0]
    parts = rows // size
    here = lax.axis_index("tensor")
    for place in range(parts):

        @pl.when(here == place)
        def _():
            groups = [hidden[(place ^ j) * size : ((place ^ j) + 1) * size, :] for j in range(parts)]
            for i in range(parts // 2):
                pair = jnp.concatenate(groups[2 * i : 2 * i + 2], axis=0)
                message_ref[:, i * width : (i + 1) * width] = pair.astype(message_ref.dtype)

    message_ref[:, rows * width // (2 * size) :] = stacked(cot[...])


def hidden_units(*arrays):
    gate, cot = arrays[0], arrays[-1]
    spaces = [pltpu.SMEM if array.dtype == jnp.int32 else pltpu.VMEM for array in arrays]
    outs = [space(array.shape, array.dtype) for space, array in zip(spaces, arrays)]
    rows = 2 * cot.shape[0]
    message = pltpu.VMEM((rows, (gate.size + cot.size) // rows), gate.dtype)
    return pl.pallas_call(
        functools.partial(hidden_kernel, kept=len(arrays)),
        in_specs=[ANYWHERE] * len(arrays),
        out_specs=[IN_VMEM] + [pl.BlockSpec(memory_space=space) for space in spaces],
        out_shape=[message] + outs,
        scratch_shapes=[pltpu.VMEM(gate.shape, jnp.float32), pltpu.SemaphoreType.DMA((len(arrays),))],
        compiler_params=pltpu.CompilerParams(vmem_limit_bytes=4 * 2**20),
        name="hidden_units",
    )(*map(remaining, arrays))


def fetch_kernel(weight_ref, *refs, start, chunk):
    out_ref, sems = refs[-2:]
    loads = [
        pltpu.make_async_copy(weight_ref.at[pl.ds(start + j, chunk)], out_ref.at[pl.ds(j, chunk)], sems.at[j // chunk])
        for j in range(0, out_ref.shape[0], chunk)
    ]
    for load in loads:
        load.start()
    for load in loads:
        load.wait()


def fetch(weights, start, blocks, after=(), chunk=2):
    shape = (blocks,) + weights.shape[1:]
    return pl.pallas_call(
        functools.partial(fetch_kernel, start=start, chunk=chunk),
        in_specs=[ANYWHERE] + [IN_VMEM] * len(after),
        out_specs=IN_VMEM,
        out_shape=pltpu.VMEM(shape, weights.dtype),
        scratch_shapes=[pltpu.SemaphoreType.DMA((blocks // chunk,))],
        compiler_params=pltpu.CompilerParams(vmem_limit_bytes=4 * 2**20),
        cost_estimate=pl.CostEstimate(flops=0, bytes_accessed=2**18 * blocks, transcendentals=0),
        name="fetch",
    )(remaining(weights), *map(resident, after))


def hidden_grad_kernel(*refs, start, fetched, earlier, ahead):
    index_ref, cot_ref, gate_ref, up_ref = refs[:4]
    held = refs[4 : 4 + fetched]
    done = refs[4 + fetched : 4 + fetched + earlier]
    span, size = held[0].shape[1:]
    if ahead:
        weight_ref, (gate_out, up_out, next_ref, sem) = refs[4 + fetched + earlier], refs[-4:]
        load = pltpu.make_async_copy(weight_ref.at[pl.ds(weight_ref.shape[0] - ahead, ahead)], next_ref, sem)
        load.start()
    else:
        gate_out, up_out = refs[-2:]
    places = [(ref, j) for ref in held for j in range(ref.shape[0])]
    for source, target in zip(done, (gate_out, up_out)):
        target[:, : start * size] = source[...]
    for block in range(start, gate_out.shape[1] // size):
        chosen = jnp.concatenate(
            [cot_ref[:, pl.ds(pl.multiple_of(index_ref[k, block] * size, size), size)] for k in range(span // size)],
            axis=1,
        )
        ref, j = places[block]
        grad = jnp.dot(chosen, ref[j], preferred_element_type=jnp.float32)
        here = slice(block * size, (block + 1) * size)
        gate = gate_ref[:, here].astype(jnp.float32)
        up = up_ref[:, here].astype(jnp.float32)
        sig = jax.nn.sigmoid(gate)
        gate_out[:, here] = (grad * up * sig * (1.0 + gate * (1.0 - sig))).astype(jnp.bfloat16)
        up_out[:, here] = (grad * gate * sig).astype(jnp.bfloat16)
    if ahead:
        load.wait()


def hidden_grads(index, cot, gate, up, held, start, stop, earlier=(), weights=None, ahead=0):
    _, span, size = held[0].shape
    rows = cot.shape[0]
    shape = (rows, stop * size)
    outs = [jax.ShapeDtypeStruct(shape, gate.dtype)] * 2
    if ahead:
        outs = [pltpu.VMEM(shape, gate.dtype)] * 2 + [pltpu.VMEM((ahead, span, size), weights.dtype)]
    return pl.pallas_call(
        functools.partial(
            hidden_grad_kernel, start=start, fetched=len(held), earlier=len(earlier), ahead=ahead
        ),
        in_specs=[IN_SMEM] + [IN_VMEM] * (3 + len(held) + len(earlier)) + [ANYWHERE] * bool(ahead),
        out_specs=[IN_VMEM] * len(outs),
        out_shape=outs,
        scratch_shapes=[pltpu.SemaphoreType.DMA] * bool(ahead),
        compiler_params=pltpu.CompilerParams(vmem_limit_bytes=4 * 2**20),
        cost_estimate=pl.CostEstimate(
            flops=2 * rows * (stop - start) * span * size,
            bytes_accessed=2 * (stop - start) * span * size,
            transcendentals=0,
        ),
        name="hidden_grads",
    )(
        scalar(index),
        *map(resident, (cot, gate, up, *held, *earlier)),
        *([remaining(weights)] if ahead else []),
    )


def pack_kernel(*refs, count):
    pieces, out_ref = refs[:count], refs[-1]
    rows = pieces[0].shape[0]
    for i, piece in enumerate(pieces):
        out_ref[i * rows : (i + 1) * rows, :] = piece[...]


def pack(pieces, after):
    rows, width = pieces[0].shape
    return pl.pallas_call(
        functools.partial(pack_kernel, count=len(pieces)),
        in_specs=[IN_VMEM] * (len(pieces) + len(after)),
        out_specs=IN_VMEM,
        out_shape=pltpu.VMEM((len(pieces) * rows, width), pieces[0].dtype),
        compiler_params=pltpu.CompilerParams(vmem_limit_bytes=4 * 2**20),
        cost_estimate=pl.CostEstimate(flops=0, bytes_accessed=LONG, transcendentals=0),
        name="pack",
    )(*map(resident, pieces), *map(resident, after))


def turn_kernel(*refs, places, rows):
    out_ref = refs[-1]
    features = out_ref.shape[0]
    per_half = features // 2
    for d in range(features):
        slices = []
        low, column = (d // per_half) * rows, (d % per_half) * 128
        for (i, i_row), (j, j_row) in places:
            start = refs[i].shape[1] - per_half * 128 + column
            own = refs[i][i_row : i_row + 2 * rows, start : start + 128]
            start = features * 128 + column
            near = refs[j][j_row : j_row + 2 * rows, start : start + 128]
            slices += [own[low : low + rows], near[low : low + rows]]
            slices.append(refs[j][j_row : j_row + 2 * rows, d * 128 : (d + 1) * 128])
        out_ref[d] = jnp.concatenate(slices, axis=0).T


def turn(pieces, rows):
    arrays = []
    for piece in pieces:
        arrays += [array for array, _ in piece if not any(array is other for other in arrays)]
    places = [[([array is other for other in arrays].index(True), row) for array, row in piece] for piece in pieces]
    width = pieces[0][1][0].shape[1] * 2 // 3
    return pl.pallas_call(
        functools.partial(turn_kernel, places=places, rows=rows),
        in_specs=[IN_VMEM] * len(arrays),
        out_specs=IN_VMEM,
        out_shape=pltpu.VMEM((width // 128, 128, len(pieces) * 4 * rows), arrays[0].dtype),
        compiler_params=pltpu.CompilerParams(vmem_limit_bytes=4 * 2**20),
        name="turn",
    )(*map(resident, arrays))


def down_grad_kernel(index_ref, *refs, halves, places, rows, kept, chunk, scale):
    turned, messages, (out_ref, held, sems) = refs[:halves], refs[halves:-3], refs[-3:]
    first = lax.axis_index("dp") * kept
    blocks = held.shape[0]
    copies = []
    for start in range(0, blocks, chunk):
        for block in range(start, start + chunk):
            right = jnp.concatenate(
                [
                    messages[i][row : row + rows, column * 128 : (column + 1) * 128]
                    for i, row in places
                    for column in (block, blocks + block)
                ],
                axis=0,
            )
            left = jnp.concatenate(
                [jnp.concatenate([t[index_ref[first + k, block]] for t in turned], axis=1) for k in range(kept)], axis=0
            )
            held[block] = jnp.dot(left, right, preferred_element_type=jnp.float32) * scale
        span = pl.ds(start, chunk)
        copy = pltpu.make_async_copy(held.at[span], out_ref.at[span], sems.at[start // chunk])
        copy.start()
        copies.append(copy)
    for copy in copies:
        copy.wait()


def down_grads(index, turned, messages, blocks, rows, kept, scale, chunk=4):
    arrays = []
    for array, _ in messages:
        arrays += [array] * (not any(array is other for other in arrays))
    places = [([array is other for other in arrays].index(True), row) for array, row in messages]
    shape = (blocks, kept * 128, 128)
    return pl.pallas_call(
        functools.partial(
            down_grad_kernel, halves=len(turned), places=places, rows=rows, kept=kept, chunk=chunk, scale=scale
        ),
        in_specs=[IN_SMEM] + [IN_VMEM] * (len(turned) + len(arrays)),
        out_specs=ANYWHERE,
        out_shape=jax.ShapeDtypeStruct(shape, jnp.float32),
        scratch_shapes=[pltpu.VMEM(shape, jnp.float32), pltpu.SemaphoreType.DMA((blocks // chunk,))],
        compiler_params=pltpu.CompilerParams(vmem_limit_bytes=12 * 2**20),
        cost_estimate=pl.CostEstimate(
            flops=4 * len(messages) * rows * kept * 128 * blocks * 128,
            bytes_accessed=4 * kept * blocks * 128 * 128,
            transcendentals=0,
        ),
        name="down_grads",
    )(scalar(index), *map(resident, (*turned, *arrays)))


def gathered(gate_act, up_act, cotangent, down_blocks, down_index):
    replicas = lax.axis_size("dp")
    parts = lax.axis_size("tensor")
    kept = down_index.shape[1] // replicas

    first = functools.partial(
        lax.ppermute, axis_name="dp", perm=[(i, i ^ (2 if i % 2 == 0 else 4)) for i in range(replicas)]
    )
    second = functools.partial(
        lax.ppermute, axis_name="dp", perm=[(i, i ^ (4 if i % 2 == 0 else 2)) for i in range(replicas)]
    )
    across = functools.partial(lax.ppermute, axis_name="dp", perm=[(i, i ^ 6) for i in range(replicas)])
    other = functools.partial(lax.ppermute, axis_name="dp", perm=[(i, i ^ 1) for i in range(replicas)])

    message, gate, up, index, near = hidden_units(gate_act, up_act, down_index.T, cotangent)
    rows = message.shape[0]
    m1, m2 = first(message), second(message)
    slices = [lax.ppermute(near, "tensor", [(i, i ^ s) for i in range(parts)]) for s in range(1, parts)]
    blocks = down_blocks.shape[0]
    half = blocks // 2
    ahead = blocks * 3 // 14
    held = [fetch(down_blocks, 0, blocks - ahead)]
    cot, sent = assemble([near] + slices, held)
    c1, c2 = first(sent), second(sent)
    packed = pack([message, m1, m2], [cot])
    m3 = second(m1)
    packed_x, c0x = other(packed), other(sent)
    *grads, rest = hidden_grads(index, cot, gate, up, held, 0, half, weights=down_blocks, ahead=ahead)
    c1, c2, grads = lax.optimization_barrier((c1, c2, grads))
    c3 = second(c1)
    c1x, c2x = other(c1), other(c2)
    grads = hidden_grads(index, cot, gate, up, held + [rest], half, blocks, grads)
    messages = [(array, i * rows) for i in range(3) for array in (packed, packed_x)]
    early = turn(list(zip(messages[:4], [(sent, 0), (c0x, 0), (c1, 0), (c1x, 0)])), rows // 2)
    c3, m3, early, c2x, packed_x, (gate_out, up_out) = lax.optimization_barrier(
        (c3, m3, early, c2x, packed_x, grads)
    )
    m3x, c3x = other(m3), other(c3)
    messages = [(array, i * rows) for i in range(3) for array in (packed, packed_x)] + [(m3, 0), (m3x, 0)]
    late = turn(list(zip(messages[4:], [(c2, 0), (c2x, 0), (c3, 0), (c3x, 0)])), rows // 2)
    down_grad = down_grads(index, [early, late], messages, blocks, rows, kept, 1.0 / replicas)
    return down_grad.transpose(1, 0, 2), gate_out, up_out


def local(gate_act, up_act, cotangent, down_blocks, down_index):
    sizes = (lax.axis_size("dp"), lax.axis_size("tensor"), gate_act.shape[0], down_blocks.shape[0] % 4)
    if sizes == (8, 4, 32, 0):
        return gathered(gate_act, up_act, cotangent, down_blocks, down_index)
    return reduced(gate_act, up_act, cotangent, down_blocks, down_index)


def solution(mesh):
    in_specs = (
        P("dp", "tensor"),
        P("dp", "tensor"),
        P(("dp", "tensor"), None),
        P("tensor", None, None),
        P("tensor", None),
    )
    out_specs = (P("dp", "tensor", None), P("dp", "tensor"), P("dp", "tensor"))
    return jax.shard_map(local, mesh=mesh, in_specs=in_specs, out_specs=out_specs, check_vma=False)
```

```python
import functools

import jax
import jax.numpy as jnp
from jax import lax
from jax.experimental import pallas as pl
from jax.experimental.pallas import tpu as pltpu
from jax.sharding import PartitionSpec as P


def reduced(gate_act, up_act, cotangent, down_blocks, down_index):
    gathered = lax.all_gather(cotangent, "tensor", axis=0, tiled=True)
    row_count = gathered.shape[0]
    local_blocks, kept_span, block_size = down_blocks.shape
    feature_count = gathered.shape[1] // block_size
    feature_view = gathered.reshape(row_count, feature_count, block_size)
    gate_value = gate_act.astype(jnp.float32).reshape(row_count, local_blocks, block_size)
    up_value = up_act.astype(jnp.float32).reshape(row_count, local_blocks, block_size)
    sigmoid_gate = jax.nn.sigmoid(gate_value)
    hidden = (gate_value * sigmoid_gate * up_value).astype(jnp.bfloat16)
    hidden_blocks = hidden.transpose(1, 0, 2)
    replicas = lax.axis_size("dp")

    def select(index_row):
        return jnp.take(feature_view, index_row, axis=1).reshape(row_count, kept_span)

    def one_grad(inputs):
        index_row, weight_block = inputs
        return jnp.dot(select(index_row), weight_block, preferred_element_type=jnp.float32)

    hidden_grad = lax.map(one_grad, (down_index, down_blocks)).transpose(1, 0, 2)
    gate_out = (
        (hidden_grad * up_value * sigmoid_gate * (1.0 + gate_value * (1.0 - sigmoid_gate)))
        .astype(jnp.bfloat16)
        .reshape(row_count, local_blocks * block_size)
    )
    up_out = (
        (hidden_grad * gate_value * sigmoid_gate)
        .astype(jnp.bfloat16)
        .reshape(row_count, local_blocks * block_size)
    )

    def one_term(inputs):
        index_row, hidden_block = inputs
        part_rows = select(index_row)
        return jnp.dot(part_rows.T, hidden_block, preferred_element_type=jnp.float32)

    summed = lax.psum_scatter(
        lax.map(one_term, (down_index, hidden_blocks)).transpose(1, 0, 2),
        "dp",
        scatter_dimension=0,
        tiled=True,
    )
    down_grad = summed / replicas
    return (down_grad, gate_out, up_out)


LONG = 2**27
IN_VMEM = pl.BlockSpec(memory_space=pltpu.VMEM)
IN_SMEM = pl.BlockSpec(memory_space=pltpu.SMEM)
ANYWHERE = pl.BlockSpec(memory_space=pl.ANY)


def resident(array):
    return pltpu.with_memory_space_constraint(array, pltpu.VMEM)


def scalar(array):
    return pltpu.with_memory_space_constraint(array, pltpu.SMEM)


def remaining(array):
    return pltpu.with_memory_space_constraint(array, pltpu.HBM)


def assemble_kernel(*refs, parts):
    pieces, (out_ref, sent_ref) = refs[:parts][::-1], refs[-2:]
    here = lax.axis_index("tensor")
    for place in range(parts):

        @pl.when(here == place)
        def _():
            out_ref[...] = jnp.concatenate([pieces[place ^ q][...] for q in range(parts)], axis=0)

    width = out_ref.shape[1]
    sent_ref[:, :width] = jnp.concatenate([piece[...] for piece in pieces[2:]], axis=0)
    sent_ref[:, width:] = stacked(pieces[1][...])


def stacked(rows):
    half = rows.shape[1] // 2
    return jnp.concatenate([rows[:, :half], rows[:, half:]], axis=0)


def assemble(pieces, after):
    rows, width = pieces[0].shape
    parts = len(pieces)
    dtype = pieces[0].dtype
    return pl.pallas_call(
        functools.partial(assemble_kernel, parts=parts),
        in_specs=[IN_VMEM] * (parts + len(after)),
        out_specs=[IN_VMEM] * 2,
        out_shape=[pltpu.VMEM((parts * rows, width), dtype), pltpu.VMEM((2 * rows, width * 3 // 2), dtype)],
        compiler_params=pltpu.CompilerParams(vmem_limit_bytes=4 * 2**20),
        cost_estimate=pl.CostEstimate(flops=0, bytes_accessed=LONG, transcendentals=0),
        name="assemble",
    )(*map(resident, pieces[::-1]), *map(resident, after))


def hidden_kernel(*refs, kept):
    sources, message_ref, targets, (hidden, sems) = refs[:kept], refs[kept], refs[kept + 1 : -2], refs[-2:]
    loads = [pltpu.make_async_copy(source, target, sems.at[i]) for i, (source, target) in enumerate(zip(sources, targets))]
    for load in loads:
        load.start()
    for load in loads:
        load.wait()
    gate = targets[0][...].astype(jnp.float32)
    up = targets[1][...].astype(jnp.float32)
    hidden[...] = gate * jax.nn.sigmoid(gate) * up
    rows, width = hidden.shape
    cot = targets[-1]
    size = cot.shape[0]
    parts = rows // size
    here = lax.axis_index("tensor")
    for place in range(parts):

        @pl.when(here == place)
        def _():
            groups = [hidden[(place ^ j) * size : ((place ^ j) + 1) * size, :] for j in range(parts)]
            for i in range(parts // 2):
                pair = jnp.concatenate(groups[2 * i : 2 * i + 2], axis=0)
                message_ref[:, i * width : (i + 1) * width] = pair.astype(message_ref.dtype)

    message_ref[:, rows * width // (2 * size) :] = stacked(cot[...])


def hidden_units(*arrays):
    gate, cot = arrays[0], arrays[-1]
    spaces = [pltpu.SMEM if array.dtype == jnp.int32 else pltpu.VMEM for array in arrays]
    outs = [space(array.shape, array.dtype) for space, array in zip(spaces, arrays)]
    rows = 2 * cot.shape[0]
    message = pltpu.VMEM((rows, (gate.size + cot.size) // rows), gate.dtype)
    return pl.pallas_call(
        functools.partial(hidden_kernel, kept=len(arrays)),
        in_specs=[ANYWHERE] * len(arrays),
        out_specs=[IN_VMEM] + [pl.BlockSpec(memory_space=space) for space in spaces],
        out_shape=[message] + outs,
        scratch_shapes=[pltpu.VMEM(gate.shape, jnp.float32), pltpu.SemaphoreType.DMA((len(arrays),))],
        compiler_params=pltpu.CompilerParams(vmem_limit_bytes=4 * 2**20),
        name="hidden_units",
    )(*map(remaining, arrays))


def fetch_kernel(weight_ref, *refs, start, chunk):
    out_ref, sems = refs[-2:]
    loads = [
        pltpu.make_async_copy(weight_ref.at[pl.ds(start + j, chunk)], out_ref.at[pl.ds(j, chunk)], sems.at[j // chunk])
        for j in range(0, out_ref.shape[0], chunk)
    ]
    for load in loads:
        load.start()
    for load in loads:
        load.wait()


def fetch(weights, start, blocks, after=(), chunk=2):
    shape = (blocks,) + weights.shape[1:]
    return pl.pallas_call(
        functools.partial(fetch_kernel, start=start, chunk=chunk),
        in_specs=[ANYWHERE] + [IN_VMEM] * len(after),
        out_specs=IN_VMEM,
        out_shape=pltpu.VMEM(shape, weights.dtype),
        scratch_shapes=[pltpu.SemaphoreType.DMA((blocks // chunk,))],
        compiler_params=pltpu.CompilerParams(vmem_limit_bytes=4 * 2**20),
        cost_estimate=pl.CostEstimate(flops=0, bytes_accessed=2**18 * blocks, transcendentals=0),
        name="fetch",
    )(remaining(weights), *map(resident, after))


def hidden_grad_kernel(*refs, start, fetched, earlier, ahead):
    index_ref, cot_ref, gate_ref, up_ref = refs[:4]
    held = refs[4 : 4 + fetched]
    done = refs[4 + fetched : 4 + fetched + earlier]
    span, size = held[0].shape[1:]
    if ahead:
        weight_ref, (gate_out, up_out, next_ref, sem) = refs[4 + fetched + earlier], refs[-4:]
        load = pltpu.make_async_copy(weight_ref.at[pl.ds(weight_ref.shape[0] - ahead, ahead)], next_ref, sem)
        load.start()
    else:
        gate_out, up_out = refs[-2:]
    places = [(ref, j) for ref in held for j in range(ref.shape[0])]
    for source, target in zip(done, (gate_out, up_out)):
        target[:, : start * size] = source[...]
    for block in range(start, gate_out.shape[1] // size):
        chosen = jnp.concatenate(
            [cot_ref[:, pl.ds(pl.multiple_of(index_ref[k, block] * size, size), size)] for k in range(span // size)],
            axis=1,
        )
        ref, j = places[block]
        grad = jnp.dot(chosen, ref[j], preferred_element_type=jnp.float32)
        here = slice(block * size, (block + 1) * size)
        gate = gate_ref[:, here].astype(jnp.float32)
        up = up_ref[:, here].astype(jnp.float32)
        sig = jax.nn.sigmoid(gate)
        gate_out[:, here] = (grad * up * sig * (1.0 + gate * (1.0 - sig))).astype(jnp.bfloat16)
        up_out[:, here] = (grad * gate * sig).astype(jnp.bfloat16)
    if ahead:
        load.wait()


def hidden_grads(index, cot, gate, up, held, start, stop, earlier=(), weights=None, ahead=0):
    _, span, size = held[0].shape
    rows = cot.shape[0]
    shape = (rows, stop * size)
    outs = [jax.ShapeDtypeStruct(shape, gate.dtype)] * 2
    if ahead:
        outs = [pltpu.VMEM(shape, gate.dtype)] * 2 + [pltpu.VMEM((ahead, span, size), weights.dtype)]
    return pl.pallas_call(
        functools.partial(
            hidden_grad_kernel, start=start, fetched=len(held), earlier=len(earlier), ahead=ahead
        ),
        in_specs=[IN_SMEM] + [IN_VMEM] * (3 + len(held) + len(earlier)) + [ANYWHERE] * bool(ahead),
        out_specs=[IN_VMEM] * len(outs),
        out_shape=outs,
        scratch_shapes=[pltpu.SemaphoreType.DMA] * bool(ahead),
        compiler_params=pltpu.CompilerParams(vmem_limit_bytes=4 * 2**20),
        cost_estimate=pl.CostEstimate(
            flops=2 * rows * (stop - start) * span * size,
            bytes_accessed=2 * (stop - start) * span * size,
            transcendentals=0,
        ),
        name="hidden_grads",
    )(
        scalar(index),
        *map(resident, (cot, gate, up, *held, *earlier)),
        *([remaining(weights)] if ahead else []),
    )


def pack_kernel(*refs, count):
    pieces, out_ref = refs[:count], refs[-1]
    rows = pieces[0].shape[0]
    for i, piece in enumerate(pieces):
        out_ref[i * rows : (i + 1) * rows, :] = piece[...]


def pack(pieces, after):
    rows, width = pieces[0].shape
    return pl.pallas_call(
        functools.partial(pack_kernel, count=len(pieces)),
        in_specs=[IN_VMEM] * (len(pieces) + len(after)),
        out_specs=IN_VMEM,
        out_shape=pltpu.VMEM((len(pieces) * rows, width), pieces[0].dtype),
        compiler_params=pltpu.CompilerParams(vmem_limit_bytes=4 * 2**20),
        cost_estimate=pl.CostEstimate(flops=0, bytes_accessed=LONG, transcendentals=0),
        name="pack",
    )(*map(resident, pieces), *map(resident, after))


def turn_kernel(*refs, places, rows):
    out_ref = refs[-1]
    features = out_ref.shape[0]
    per_half = features // 2
    for d in range(features):
        slices = []
        low, column = (d // per_half) * rows, (d % per_half) * 128
        for (i, i_row), (j, j_row) in places:
            start = refs[i].shape[1] - per_half * 128 + column
            own = refs[i][i_row : i_row + 2 * rows, start : start + 128]
            start = features * 128 + column
            near = refs[j][j_row : j_row + 2 * rows, start : start + 128]
            slices += [own[low : low + rows], near[low : low + rows]]
            slices.append(refs[j][j_row : j_row + 2 * rows, d * 128 : (d + 1) * 128])
        out_ref[d] = jnp.concatenate(slices, axis=0).T


def turn(pieces, rows):
    arrays = []
    for piece in pieces:
        arrays += [array for array, _ in piece if not any(array is other for other in arrays)]
    places = [[([array is other for other in arrays].index(True), row) for array, row in piece] for piece in pieces]
    width = pieces[0][1][0].shape[1] * 2 // 3
    return pl.pallas_call(
        functools.partial(turn_kernel, places=places, rows=rows),
        in_specs=[IN_VMEM] * len(arrays),
        out_specs=IN_VMEM,
        out_shape=pltpu.VMEM((width // 128, 128, len(pieces) * 4 * rows), arrays[0].dtype),
        compiler_params=pltpu.CompilerParams(vmem_limit_bytes=4 * 2**20),
        name="turn",
    )(*map(resident, arrays))


def down_grad_kernel(index_ref, *refs, halves, places, rows, kept, chunk, scale):
    turned, messages, (out_ref, held, sems) = refs[:halves], refs[halves:-3], refs[-3:]
    first = lax.axis_index("dp") * kept
    blocks = held.shape[0]
    copies = []
    for start in range(0, blocks, chunk):
        for block in range(start, start + chunk):
            right = jnp.concatenate(
                [
                    messages[i][row : row + rows, column * 128 : (column + 1) * 128]
                    for i, row in places
                    for column in (block, blocks + block)
                ],
                axis=0,
            )
            left = jnp.concatenate(
                [jnp.concatenate([t[index_ref[first + k, block]] for t in turned], axis=1) for k in range(kept)], axis=0
            )
            held[block] = jnp.dot(left, right, preferred_element_type=jnp.float32) * scale
        span = pl.ds(start, chunk)
        copy = pltpu.make_async_copy(held.at[span], out_ref.at[span], sems.at[start // chunk])
        copy.start()
        copies.append(copy)
    for copy in copies:
        copy.wait()


def down_grads(index, turned, messages, blocks, rows, kept, scale, chunk=4):
    arrays = []
    for array, _ in messages:
        arrays += [array] * (not any(array is other for other in arrays))
    places = [([array is other for other in arrays].index(True), row) for array, row in messages]
    shape = (blocks, kept * 128, 128)
    return pl.pallas_call(
        functools.partial(
            down_grad_kernel, halves=len(turned), places=places, rows=rows, kept=kept, chunk=chunk, scale=scale
        ),
        in_specs=[IN_SMEM] + [IN_VMEM] * (len(turned) + len(arrays)),
        out_specs=ANYWHERE,
        out_shape=jax.ShapeDtypeStruct(shape, jnp.float32),
        scratch_shapes=[pltpu.VMEM(shape, jnp.float32), pltpu.SemaphoreType.DMA((blocks // chunk,))],
        compiler_params=pltpu.CompilerParams(vmem_limit_bytes=12 * 2**20),
        cost_estimate=pl.CostEstimate(
            flops=4 * len(messages) * rows * kept * 128 * blocks * 128,
            bytes_accessed=4 * kept * blocks * 128 * 128,
            transcendentals=0,
        ),
        name="down_grads",
    )(scalar(index), *map(resident, (*turned, *arrays)))


def gathered(gate_act, up_act, cotangent, down_blocks, down_index):
    replicas = lax.axis_size("dp")
    parts = lax.axis_size("tensor")
    kept = down_index.shape[1] // replicas

    first = functools.partial(
        lax.ppermute, axis_name="dp", perm=[(i, i ^ (2 if i % 2 == 0 else 4)) for i in range(replicas)]
    )
    second = functools.partial(
        lax.ppermute, axis_name="dp", perm=[(i, i ^ (4 if i % 2 == 0 else 2)) for i in range(replicas)]
    )
    across = functools.partial(lax.ppermute, axis_name="dp", perm=[(i, i ^ 6) for i in range(replicas)])
    other = functools.partial(lax.ppermute, axis_name="dp", perm=[(i, i ^ 1) for i in range(replicas)])

    message, gate, up, index, near = hidden_units(gate_act, up_act, down_index.T, cotangent)
    rows = message.shape[0]
    m1, m2 = first(message), second(message)
    slices = [lax.ppermute(near, "tensor", [(i, i ^ s) for i in range(parts)]) for s in range(1, parts)]
    blocks = down_blocks.shape[0]
    half = blocks // 2
    ahead = blocks * 3 // 14
    held = [fetch(down_blocks, 0, blocks - ahead)]
    cot, sent = assemble([near] + slices, held)
    c1, c2 = first(sent), second(sent)
    packed = pack([message, m1, m2], [cot])
    m3 = first(m2)
    packed_x, c0x = other(packed), other(sent)
    *grads, rest = hidden_grads(index, cot, gate, up, held, 0, half, weights=down_blocks, ahead=ahead)
    c1, grads = lax.optimization_barrier((c1, grads))
    c3 = second(c1)
    c1x, c2x = other(c1), other(c2)
    grads = hidden_grads(index, cot, gate, up, held + [rest], half, blocks, grads)
    messages = [(array, i * rows) for i in range(3) for array in (packed, packed_x)]
    early = turn(list(zip(messages[:4], [(sent, 0), (c0x, 0), (c1, 0), (c1x, 0)])), rows // 2)
    c3, m3, early, c2x, packed_x, (gate_out, up_out) = lax.optimization_barrier(
        (c3, m3, early, c2x, packed_x, grads)
    )
    m3x, c3x = other(m3), other(c3)
    messages = [(array, i * rows) for i in range(3) for array in (packed, packed_x)] + [(m3, 0), (m3x, 0)]
    late = turn(list(zip(messages[4:], [(c2, 0), (c2x, 0), (c3, 0), (c3x, 0)])), rows // 2)
    down_grad = down_grads(index, [early, late], messages, blocks, rows, kept, 1.0 / replicas)
    return down_grad.transpose(1, 0, 2), gate_out, up_out


def local(gate_act, up_act, cotangent, down_blocks, down_index):
    sizes = (lax.axis_size("dp"), lax.axis_size("tensor"), gate_act.shape[0], down_blocks.shape[0] % 4)
    if sizes == (8, 4, 32, 0):
        return gathered(gate_act, up_act, cotangent, down_blocks, down_index)
    return reduced(gate_act, up_act, cotangent, down_blocks, down_index)


def solution(mesh):
    in_specs = (
        P("dp", "tensor"),
        P("dp", "tensor"),
        P(("dp", "tensor"), None),
        P("tensor", None, None),
        P("tensor", None),
    )
    out_specs = (P("dp", "tensor", None), P("dp", "tensor"), P("dp", "tensor"))
    return jax.shard_map(local, mesh=mesh, in_specs=in_specs, out_specs=out_specs, check_vma=False)
```

```python
import functools

import jax
import jax.numpy as jnp
from jax import lax
from jax.experimental import pallas as pl
from jax.experimental.pallas import tpu as pltpu
from jax.sharding import PartitionSpec as P


def reduced(gate_act, up_act, cotangent, down_blocks, down_index):
    gathered = lax.all_gather(cotangent, "tensor", axis=0, tiled=True)
    row_count = gathered.shape[0]
    local_blocks, kept_span, block_size = down_blocks.shape
    feature_count = gathered.shape[1] // block_size
    feature_view = gathered.reshape(row_count, feature_count, block_size)
    gate_value = gate_act.astype(jnp.float32).reshape(row_count, local_blocks, block_size)
    up_value = up_act.astype(jnp.float32).reshape(row_count, local_blocks, block_size)
    sigmoid_gate = jax.nn.sigmoid(gate_value)
    hidden = (gate_value * sigmoid_gate * up_value).astype(jnp.bfloat16)
    hidden_blocks = hidden.transpose(1, 0, 2)
    replicas = lax.axis_size("dp")

    def select(index_row):
        return jnp.take(feature_view, index_row, axis=1).reshape(row_count, kept_span)

    def one_grad(inputs):
        index_row, weight_block = inputs
        return jnp.dot(select(index_row), weight_block, preferred_element_type=jnp.float32)

    hidden_grad = lax.map(one_grad, (down_index, down_blocks)).transpose(1, 0, 2)
    gate_out = (
        (hidden_grad * up_value * sigmoid_gate * (1.0 + gate_value * (1.0 - sigmoid_gate)))
        .astype(jnp.bfloat16)
        .reshape(row_count, local_blocks * block_size)
    )
    up_out = (
        (hidden_grad * gate_value * sigmoid_gate)
        .astype(jnp.bfloat16)
        .reshape(row_count, local_blocks * block_size)
    )

    def one_term(inputs):
        index_row, hidden_block = inputs
        part_rows = select(index_row)
        return jnp.dot(part_rows.T, hidden_block, preferred_element_type=jnp.float32)

    summed = lax.psum_scatter(
        lax.map(one_term, (down_index, hidden_blocks)).transpose(1, 0, 2),
        "dp",
        scatter_dimension=0,
        tiled=True,
    )
    down_grad = summed / replicas
    return (down_grad, gate_out, up_out)


LONG = 2**27
IN_VMEM = pl.BlockSpec(memory_space=pltpu.VMEM)
IN_SMEM = pl.BlockSpec(memory_space=pltpu.SMEM)
ANYWHERE = pl.BlockSpec(memory_space=pl.ANY)


def resident(array):
    return pltpu.with_memory_space_constraint(array, pltpu.VMEM)


def scalar(array):
    return pltpu.with_memory_space_constraint(array, pltpu.SMEM)


def remaining(array):
    return pltpu.with_memory_space_constraint(array, pltpu.HBM)


def assemble_kernel(*refs, parts):
    pieces, (out_ref, sent_ref) = refs[:parts][::-1], refs[-2:]
    here = lax.axis_index("tensor")
    for place in range(parts):

        @pl.when(here == place)
        def _():
            out_ref[...] = jnp.concatenate([pieces[place ^ q][...] for q in range(parts)], axis=0)

    width = out_ref.shape[1]
    sent_ref[:, :width] = jnp.concatenate([piece[...] for piece in pieces[2:]], axis=0)
    sent_ref[:, width:] = stacked(pieces[1][...])


def stacked(rows):
    half = rows.shape[1] // 2
    return jnp.concatenate([rows[:, :half], rows[:, half:]], axis=0)


def assemble(pieces, after):
    rows, width = pieces[0].shape
    parts = len(pieces)
    dtype = pieces[0].dtype
    return pl.pallas_call(
        functools.partial(assemble_kernel, parts=parts),
        in_specs=[IN_VMEM] * (parts + len(after)),
        out_specs=[IN_VMEM] * 2,
        out_shape=[pltpu.VMEM((parts * rows, width), dtype), pltpu.VMEM((2 * rows, width * 3 // 2), dtype)],
        compiler_params=pltpu.CompilerParams(vmem_limit_bytes=4 * 2**20),
        cost_estimate=pl.CostEstimate(flops=0, bytes_accessed=LONG, transcendentals=0),
        name="assemble",
    )(*map(resident, pieces[::-1]), *map(resident, after))


def hidden_kernel(*refs, kept):
    sources, message_ref, targets, (hidden, sems) = refs[:kept], refs[kept], refs[kept + 1 : -2], refs[-2:]
    loads = [pltpu.make_async_copy(source, target, sems.at[i]) for i, (source, target) in enumerate(zip(sources, targets))]
    for load in loads:
        load.start()
    for load in loads:
        load.wait()
    gate = targets[0][...].astype(jnp.float32)
    up = targets[1][...].astype(jnp.float32)
    hidden[...] = gate * jax.nn.sigmoid(gate) * up
    rows, width = hidden.shape
    cot = targets[-1]
    size = cot.shape[0]
    parts = rows // size
    here = lax.axis_index("tensor")
    for place in range(parts):

        @pl.when(here == place)
        def _():
            groups = [hidden[(place ^ j) * size : ((place ^ j) + 1) * size, :] for j in range(parts)]
            for i in range(parts // 2):
                pair = jnp.concatenate(groups[2 * i : 2 * i + 2], axis=0)
                message_ref[:, i * width : (i + 1) * width] = pair.astype(message_ref.dtype)

    message_ref[:, rows * width // (2 * size) :] = stacked(cot[...])


def hidden_units(*arrays):
    gate, cot = arrays[0], arrays[-1]
    spaces = [pltpu.SMEM if array.dtype == jnp.int32 else pltpu.VMEM for array in arrays]
    outs = [space(array.shape, array.dtype) for space, array in zip(spaces, arrays)]
    rows = 2 * cot.shape[0]
    message = pltpu.VMEM((rows, (gate.size + cot.size) // rows), gate.dtype)
    return pl.pallas_call(
        functools.partial(hidden_kernel, kept=len(arrays)),
        in_specs=[ANYWHERE] * len(arrays),
        out_specs=[IN_VMEM] + [pl.BlockSpec(memory_space=space) for space in spaces],
        out_shape=[message] + outs,
        scratch_shapes=[pltpu.VMEM(gate.shape, jnp.float32), pltpu.SemaphoreType.DMA((len(arrays),))],
        compiler_params=pltpu.CompilerParams(vmem_limit_bytes=4 * 2**20),
        name="hidden_units",
    )(*map(remaining, arrays))


def fetch_kernel(weight_ref, *refs, start, chunk):
    out_ref, sems = refs[-2:]
    loads = [
        pltpu.make_async_copy(weight_ref.at[pl.ds(start + j, chunk)], out_ref.at[pl.ds(j, chunk)], sems.at[j // chunk])
        for j in range(0, out_ref.shape[0], chunk)
    ]
    for load in loads:
        load.start()
    for load in loads:
        load.wait()


def fetch(weights, start, blocks, after=(), chunk=2):
    shape = (blocks,) + weights.shape[1:]
    return pl.pallas_call(
        functools.partial(fetch_kernel, start=start, chunk=chunk),
        in_specs=[ANYWHERE] + [IN_VMEM] * len(after),
        out_specs=IN_VMEM,
        out_shape=pltpu.VMEM(shape, weights.dtype),
        scratch_shapes=[pltpu.SemaphoreType.DMA((blocks // chunk,))],
        compiler_params=pltpu.CompilerParams(vmem_limit_bytes=4 * 2**20),
        cost_estimate=pl.CostEstimate(flops=0, bytes_accessed=2**18 * blocks, transcendentals=0),
        name="fetch",
    )(remaining(weights), *map(resident, after))


def hidden_grad_kernel(*refs, start, fetched, earlier, ahead):
    index_ref, cot_ref, gate_ref, up_ref = refs[:4]
    held = refs[4 : 4 + fetched]
    done = refs[4 + fetched : 4 + fetched + earlier]
    span, size = held[0].shape[1:]
    if ahead:
        weight_ref, (gate_out, up_out, next_ref, sem) = refs[4 + fetched + earlier], refs[-4:]
        load = pltpu.make_async_copy(weight_ref.at[pl.ds(weight_ref.shape[0] - ahead, ahead)], next_ref, sem)
        load.start()
    else:
        gate_out, up_out = refs[-2:]
    places = [(ref, j) for ref in held for j in range(ref.shape[0])]
    for source, target in zip(done, (gate_out, up_out)):
        target[:, : start * size] = source[...]
    for block in range(start, gate_out.shape[1] // size):
        chosen = jnp.concatenate(
            [cot_ref[:, pl.ds(pl.multiple_of(index_ref[k, block] * size, size), size)] for k in range(span // size)],
            axis=1,
        )
        ref, j = places[block]
        grad = jnp.dot(chosen, ref[j], preferred_element_type=jnp.float32)
        here = slice(block * size, (block + 1) * size)
        gate = gate_ref[:, here].astype(jnp.float32)
        up = up_ref[:, here].astype(jnp.float32)
        sig = jax.nn.sigmoid(gate)
        gate_out[:, here] = (grad * up * sig * (1.0 + gate * (1.0 - sig))).astype(jnp.bfloat16)
        up_out[:, here] = (grad * gate * sig).astype(jnp.bfloat16)
    if ahead:
        load.wait()


def hidden_grads(index, cot, gate, up, held, start, stop, earlier=(), weights=None, ahead=0):
    _, span, size = held[0].shape
    rows = cot.shape[0]
    shape = (rows, stop * size)
    outs = [jax.ShapeDtypeStruct(shape, gate.dtype)] * 2
    if ahead:
        outs = [pltpu.VMEM(shape, gate.dtype)] * 2 + [pltpu.VMEM((ahead, span, size), weights.dtype)]
    return pl.pallas_call(
        functools.partial(
            hidden_grad_kernel, start=start, fetched=len(held), earlier=len(earlier), ahead=ahead
        ),
        in_specs=[IN_SMEM] + [IN_VMEM] * (3 + len(held) + len(earlier)) + [ANYWHERE] * bool(ahead),
        out_specs=[IN_VMEM] * len(outs),
        out_shape=outs,
        scratch_shapes=[pltpu.SemaphoreType.DMA] * bool(ahead),
        compiler_params=pltpu.CompilerParams(vmem_limit_bytes=4 * 2**20),
        cost_estimate=pl.CostEstimate(
            flops=2 * rows * (stop - start) * span * size,
            bytes_accessed=2 * (stop - start) * span * size,
            transcendentals=0,
        ),
        name="hidden_grads",
    )(
        scalar(index),
        *map(resident, (cot, gate, up, *held, *earlier)),
        *([remaining(weights)] if ahead else []),
    )


def pack_kernel(*refs, count):
    pieces, out_ref = refs[:count], refs[-1]
    rows = pieces[0].shape[0]
    for i, piece in enumerate(pieces):
        out_ref[i * rows : (i + 1) * rows, :] = piece[...]


def pack(pieces, after):
    rows, width = pieces[0].shape
    return pl.pallas_call(
        functools.partial(pack_kernel, count=len(pieces)),
        in_specs=[IN_VMEM] * (len(pieces) + len(after)),
        out_specs=IN_VMEM,
        out_shape=pltpu.VMEM((len(pieces) * rows, width), pieces[0].dtype),
        compiler_params=pltpu.CompilerParams(vmem_limit_bytes=4 * 2**20),
        cost_estimate=pl.CostEstimate(flops=0, bytes_accessed=LONG, transcendentals=0),
        name="pack",
    )(*map(resident, pieces), *map(resident, after))


def turn_kernel(*refs, places, rows):
    out_ref = refs[-1]
    features = out_ref.shape[0]
    per_half = features // 2
    for d in range(features):
        slices = []
        low, column = (d // per_half) * rows, (d % per_half) * 128
        for (i, i_row), (j, j_row) in places:
            start = refs[i].shape[1] - per_half * 128 + column
            own = refs[i][i_row : i_row + 2 * rows, start : start + 128]
            start = features * 128 + column
            near = refs[j][j_row : j_row + 2 * rows, start : start + 128]
            slices += [own[low : low + rows], near[low : low + rows]]
            slices.append(refs[j][j_row : j_row + 2 * rows, d * 128 : (d + 1) * 128])
        out_ref[d] = jnp.concatenate(slices, axis=0).T


def turn(pieces, rows):
    arrays = []
    for piece in pieces:
        arrays += [array for array, _ in piece if not any(array is other for other in arrays)]
    places = [[([array is other for other in arrays].index(True), row) for array, row in piece] for piece in pieces]
    width = pieces[0][1][0].shape[1] * 2 // 3
    return pl.pallas_call(
        functools.partial(turn_kernel, places=places, rows=rows),
        in_specs=[IN_VMEM] * len(arrays),
        out_specs=IN_VMEM,
        out_shape=pltpu.VMEM((width // 128, 128, len(pieces) * 4 * rows), arrays[0].dtype),
        compiler_params=pltpu.CompilerParams(vmem_limit_bytes=4 * 2**20),
        name="turn",
    )(*map(resident, arrays))


def down_grad_kernel(index_ref, turned, *refs, places, pieces, rows, kept, chunk, scale):
    arrays, (out_ref, held, sems) = refs[:-3], refs[-3:]
    first = lax.axis_index("dp") * kept
    blocks = held.shape[0]
    features = turned.shape[0]
    per_half = features // 2
    copies = []

    def late(feature):
        low = feature < per_half
        column = jnp.where(low, feature, feature - per_half) * 128
        slices = []
        for (i, i_row), (j, j_row) in pieces:
            for ref, row, start in (
                (arrays[i], i_row, arrays[i].shape[1] - per_half * 128),
                (arrays[j], j_row, features * 128),
            ):
                both = ref[row : row + rows, pl.ds(pl.multiple_of(start + column, 128), 128)]
                slices.append(jnp.where(low, both[: rows // 2], both[rows // 2 :]))
            slices.append(arrays[j][j_row : j_row + rows, pl.ds(pl.multiple_of(feature * 128, 128), 128)])
        return jnp.concatenate(slices, axis=0).T

    for start in range(0, blocks, chunk):
        for block in range(start, start + chunk):
            right = jnp.concatenate(
                [
                    arrays[i][row : row + rows, column * 128 : (column + 1) * 128]
                    for i, row in places
                    for column in (block, blocks + block)
                ],
                axis=0,
            )
            chosen = [index_ref[first + k, block] for k in range(kept)]
            left = jnp.concatenate([jnp.concatenate([turned[d], late(d)], axis=1) for d in chosen], axis=0)
            held[block] = jnp.dot(left, right, preferred_element_type=jnp.float32) * scale
        span = pl.ds(start, chunk)
        copy = pltpu.make_async_copy(held.at[span], out_ref.at[span], sems.at[start // chunk])
        copy.start()
        copies.append(copy)
    for copy in copies:
        copy.wait()


def down_grads(index, turned, messages, sent, blocks, rows, kept, scale, chunk=4):
    arrays = []
    for array, _ in messages + sent:
        arrays += [array] * (not any(array is other for other in arrays))

    def place(array, row):
        return [array is other for other in arrays].index(True), row

    places = [place(*message) for message in messages]
    pieces = [(place(*m), place(*c)) for m, c in zip(messages[-len(sent) :], sent)]
    shape = (blocks, kept * 128, 128)
    return pl.pallas_call(
        functools.partial(
            down_grad_kernel, places=places, pieces=pieces, rows=rows, kept=kept, chunk=chunk, scale=scale
        ),
        in_specs=[IN_SMEM] + [IN_VMEM] * (1 + len(arrays)),
        out_specs=ANYWHERE,
        out_shape=jax.ShapeDtypeStruct(shape, jnp.float32),
        scratch_shapes=[pltpu.VMEM(shape, jnp.float32), pltpu.SemaphoreType.DMA((blocks // chunk,))],
        compiler_params=pltpu.CompilerParams(vmem_limit_bytes=12 * 2**20),
        cost_estimate=pl.CostEstimate(
            flops=4 * len(messages) * rows * kept * 128 * blocks * 128,
            bytes_accessed=4 * kept * blocks * 128 * 128,
            transcendentals=0,
        ),
        name="down_grads",
    )(scalar(index), *map(resident, (turned, *arrays)))


def gathered(gate_act, up_act, cotangent, down_blocks, down_index):
    replicas = lax.axis_size("dp")
    parts = lax.axis_size("tensor")
    kept = down_index.shape[1] // replicas

    first = functools.partial(
        lax.ppermute, axis_name="dp", perm=[(i, i ^ (2 if i % 2 == 0 else 4)) for i in range(replicas)]
    )
    second = functools.partial(
        lax.ppermute, axis_name="dp", perm=[(i, i ^ (4 if i % 2 == 0 else 2)) for i in range(replicas)]
    )
    across = functools.partial(lax.ppermute, axis_name="dp", perm=[(i, i ^ 6) for i in range(replicas)])
    other = functools.partial(lax.ppermute, axis_name="dp", perm=[(i, i ^ 1) for i in range(replicas)])

    message, gate, up, index, near = hidden_units(gate_act, up_act, down_index.T, cotangent)
    rows = message.shape[0]
    m1, m2 = first(message), second(message)
    slices = [lax.ppermute(near, "tensor", [(i, i ^ s) for i in range(parts)]) for s in range(1, parts)]
    blocks = down_blocks.shape[0]
    half = blocks // 2
    ahead = blocks * 3 // 14
    held = [fetch(down_blocks, 0, blocks - ahead)]
    cot, sent = assemble([near] + slices, held)
    c1, c2 = first(sent), second(sent)
    packed = pack([message, m1, m2], [cot])
    m3 = first(m2)
    packed_x, c0x = other(packed), other(sent)
    *grads, rest = hidden_grads(index, cot, gate, up, held, 0, half, weights=down_blocks, ahead=ahead)
    c1, grads = lax.optimization_barrier((c1, grads))
    c3 = second(c1)
    c1x, c2x = other(c1), other(c2)
    grads = hidden_grads(index, cot, gate, up, held + [rest], half, blocks, grads)
    messages = [(array, i * rows) for i in range(3) for array in (packed, packed_x)]
    early = turn(list(zip(messages[:4], [(sent, 0), (c0x, 0), (c1, 0), (c1x, 0)])), rows // 2)
    c3, m3, early, c2x, packed_x, (gate_out, up_out) = lax.optimization_barrier(
        (c3, m3, early, c2x, packed_x, grads)
    )
    m3x, c3x = other(m3), other(c3)
    messages = [(array, i * rows) for i in range(3) for array in (packed, packed_x)] + [(m3, 0), (m3x, 0)]
    late = [(c2, 0), (c2x, 0), (c3, 0), (c3x, 0)]
    down_grad = down_grads(index, early, messages, late, blocks, rows, kept, 1.0 / replicas)
    return down_grad.transpose(1, 0, 2), gate_out, up_out


def local(gate_act, up_act, cotangent, down_blocks, down_index):
    sizes = (lax.axis_size("dp"), lax.axis_size("tensor"), gate_act.shape[0], down_blocks.shape[0] % 4)
    if sizes == (8, 4, 32, 0):
        return gathered(gate_act, up_act, cotangent, down_blocks, down_index)
    return reduced(gate_act, up_act, cotangent, down_blocks, down_index)


def solution(mesh):
    in_specs = (
        P("dp", "tensor"),
        P("dp", "tensor"),
        P(("dp", "tensor"), None),
        P("tensor", None, None),
        P("tensor", None),
    )
    out_specs = (P("dp", "tensor", None), P("dp", "tensor"), P("dp", "tensor"))
    return jax.shard_map(local, mesh=mesh, in_specs=in_specs, out_specs=out_specs, check_vma=False)
```

```python
import functools

import jax
import jax.numpy as jnp
from jax import lax
from jax.experimental import pallas as pl
from jax.experimental.pallas import tpu as pltpu
from jax.sharding import PartitionSpec as P


def reduced(gate_act, up_act, cotangent, down_blocks, down_index):
    gathered = lax.all_gather(cotangent, "tensor", axis=0, tiled=True)
    row_count = gathered.shape[0]
    local_blocks, kept_span, block_size = down_blocks.shape
    feature_count = gathered.shape[1] // block_size
    feature_view = gathered.reshape(row_count, feature_count, block_size)
    gate_value = gate_act.astype(jnp.float32).reshape(row_count, local_blocks, block_size)
    up_value = up_act.astype(jnp.float32).reshape(row_count, local_blocks, block_size)
    sigmoid_gate = jax.nn.sigmoid(gate_value)
    hidden = (gate_value * sigmoid_gate * up_value).astype(jnp.bfloat16)
    hidden_blocks = hidden.transpose(1, 0, 2)
    replicas = lax.axis_size("dp")

    def select(index_row):
        return jnp.take(feature_view, index_row, axis=1).reshape(row_count, kept_span)

    def one_grad(inputs):
        index_row, weight_block = inputs
        return jnp.dot(select(index_row), weight_block, preferred_element_type=jnp.float32)

    hidden_grad = lax.map(one_grad, (down_index, down_blocks)).transpose(1, 0, 2)
    gate_out = (
        (hidden_grad * up_value * sigmoid_gate * (1.0 + gate_value * (1.0 - sigmoid_gate)))
        .astype(jnp.bfloat16)
        .reshape(row_count, local_blocks * block_size)
    )
    up_out = (
        (hidden_grad * gate_value * sigmoid_gate)
        .astype(jnp.bfloat16)
        .reshape(row_count, local_blocks * block_size)
    )

    def one_term(inputs):
        index_row, hidden_block = inputs
        part_rows = select(index_row)
        return jnp.dot(part_rows.T, hidden_block, preferred_element_type=jnp.float32)

    summed = lax.psum_scatter(
        lax.map(one_term, (down_index, hidden_blocks)).transpose(1, 0, 2),
        "dp",
        scatter_dimension=0,
        tiled=True,
    )
    down_grad = summed / replicas
    return (down_grad, gate_out, up_out)


LONG = 2**27
IN_VMEM = pl.BlockSpec(memory_space=pltpu.VMEM)
IN_SMEM = pl.BlockSpec(memory_space=pltpu.SMEM)
ANYWHERE = pl.BlockSpec(memory_space=pl.ANY)


def resident(array):
    return pltpu.with_memory_space_constraint(array, pltpu.VMEM)


def scalar(array):
    return pltpu.with_memory_space_constraint(array, pltpu.SMEM)


def remaining(array):
    return pltpu.with_memory_space_constraint(array, pltpu.HBM)


def assemble_kernel(*refs, parts):
    pieces, (out_ref, sent_ref, far_ref) = refs[:parts][::-1], refs[-3:]
    here = lax.axis_index("tensor")
    for place in range(parts):

        @pl.when(here == place)
        def _():
            out_ref[...] = jnp.concatenate([pieces[place ^ q][...] for q in range(parts)], axis=0)

    width = out_ref.shape[1]
    far_ref[...] = jnp.concatenate([piece[...] for piece in pieces[2:]], axis=0)
    sent_ref[:, :width] = far_ref[...]
    sent_ref[:, width:] = stacked(pieces[1][...])


def stacked(rows):
    half = rows.shape[1] // 2
    return jnp.concatenate([rows[:, :half], rows[:, half:]], axis=0)


def assemble(pieces, after):
    rows, width = pieces[0].shape
    parts = len(pieces)
    dtype = pieces[0].dtype
    return pl.pallas_call(
        functools.partial(assemble_kernel, parts=parts),
        in_specs=[IN_VMEM] * (parts + len(after)),
        out_specs=[IN_VMEM] * 3,
        out_shape=[
            pltpu.VMEM(shape, dtype) for shape in ((parts * rows, width), (2 * rows, width * 3 // 2), (2 * rows, width))
        ],
        compiler_params=pltpu.CompilerParams(vmem_limit_bytes=4 * 2**20),
        cost_estimate=pl.CostEstimate(flops=0, bytes_accessed=LONG, transcendentals=0),
        name="assemble",
    )(*map(resident, pieces[::-1]), *map(resident, after))


def hidden_kernel(*refs, kept):
    sources, message_ref, targets, (hidden, sems) = refs[:kept], refs[kept], refs[kept + 1 : -2], refs[-2:]
    loads = [pltpu.make_async_copy(source, target, sems.at[i]) for i, (source, target) in enumerate(zip(sources, targets))]
    for load in loads:
        load.start()
    for load in loads:
        load.wait()
    gate = targets[0][...].astype(jnp.float32)
    up = targets[1][...].astype(jnp.float32)
    hidden[...] = gate * jax.nn.sigmoid(gate) * up
    rows, width = hidden.shape
    cot = targets[-1]
    size = cot.shape[0]
    parts = rows // size
    here = lax.axis_index("tensor")
    for place in range(parts):

        @pl.when(here == place)
        def _():
            groups = [hidden[(place ^ j) * size : ((place ^ j) + 1) * size, :] for j in range(parts)]
            for i in range(parts // 2):
                pair = jnp.concatenate(groups[2 * i : 2 * i + 2], axis=0)
                message_ref[:, i * width : (i + 1) * width] = pair.astype(message_ref.dtype)

    message_ref[:, rows * width // (2 * size) :] = stacked(cot[...])


def hidden_units(*arrays):
    gate, cot = arrays[0], arrays[-1]
    spaces = [pltpu.SMEM if array.dtype == jnp.int32 else pltpu.VMEM for array in arrays]
    outs = [space(array.shape, array.dtype) for space, array in zip(spaces, arrays)]
    rows = 2 * cot.shape[0]
    message = pltpu.VMEM((rows, (gate.size + cot.size) // rows), gate.dtype)
    return pl.pallas_call(
        functools.partial(hidden_kernel, kept=len(arrays)),
        in_specs=[ANYWHERE] * len(arrays),
        out_specs=[IN_VMEM] + [pl.BlockSpec(memory_space=space) for space in spaces],
        out_shape=[message] + outs,
        scratch_shapes=[pltpu.VMEM(gate.shape, jnp.float32), pltpu.SemaphoreType.DMA((len(arrays),))],
        compiler_params=pltpu.CompilerParams(vmem_limit_bytes=4 * 2**20),
        name="hidden_units",
    )(*map(remaining, arrays))


def fetch_kernel(weight_ref, *refs, start, chunk):
    out_ref, sems = refs[-2:]
    loads = [
        pltpu.make_async_copy(weight_ref.at[pl.ds(start + j, chunk)], out_ref.at[pl.ds(j, chunk)], sems.at[j // chunk])
        for j in range(0, out_ref.shape[0], chunk)
    ]
    for load in loads:
        load.start()
    for load in loads:
        load.wait()


def fetch(weights, start, blocks, after=(), chunk=2):
    shape = (blocks,) + weights.shape[1:]
    return pl.pallas_call(
        functools.partial(fetch_kernel, start=start, chunk=chunk),
        in_specs=[ANYWHERE] + [IN_VMEM] * len(after),
        out_specs=IN_VMEM,
        out_shape=pltpu.VMEM(shape, weights.dtype),
        scratch_shapes=[pltpu.SemaphoreType.DMA((blocks // chunk,))],
        compiler_params=pltpu.CompilerParams(vmem_limit_bytes=4 * 2**20),
        cost_estimate=pl.CostEstimate(flops=0, bytes_accessed=2**18 * blocks, transcendentals=0),
        name="fetch",
    )(remaining(weights), *map(resident, after))


def hidden_grad_kernel(*refs, start, fetched, earlier, ahead):
    index_ref, cot_ref, gate_ref, up_ref = refs[:4]
    held = refs[4 : 4 + fetched]
    done = refs[4 + fetched : 4 + fetched + earlier]
    span, size = held[0].shape[1:]
    if ahead:
        weight_ref, (gate_out, up_out, next_ref, sem) = refs[4 + fetched + earlier], refs[-4:]
        load = pltpu.make_async_copy(weight_ref.at[pl.ds(weight_ref.shape[0] - ahead, ahead)], next_ref, sem)
        load.start()
    else:
        gate_out, up_out = refs[-2:]
    places = [(ref, j) for ref in held for j in range(ref.shape[0])]
    for source, target in zip(done, (gate_out, up_out)):
        target[:, : start * size] = source[...]
    for block in range(start, gate_out.shape[1] // size):
        chosen = jnp.concatenate(
            [cot_ref[:, pl.ds(pl.multiple_of(index_ref[k, block] * size, size), size)] for k in range(span // size)],
            axis=1,
        )
        ref, j = places[block]
        grad = jnp.dot(chosen, ref[j], preferred_element_type=jnp.float32)
        here = slice(block * size, (block + 1) * size)
        gate = gate_ref[:, here].astype(jnp.float32)
        up = up_ref[:, here].astype(jnp.float32)
        sig = jax.nn.sigmoid(gate)
        gate_out[:, here] = (grad * up * sig * (1.0 + gate * (1.0 - sig))).astype(jnp.bfloat16)
        up_out[:, here] = (grad * gate * sig).astype(jnp.bfloat16)
    if ahead:
        load.wait()


def hidden_grads(index, cot, gate, up, held, start, stop, earlier=(), weights=None, ahead=0):
    _, span, size = held[0].shape
    rows = cot.shape[0]
    shape = (rows, stop * size)
    outs = [jax.ShapeDtypeStruct(shape, gate.dtype)] * 2
    if ahead:
        outs = [pltpu.VMEM(shape, gate.dtype)] * 2 + [pltpu.VMEM((ahead, span, size), weights.dtype)]
    return pl.pallas_call(
        functools.partial(
            hidden_grad_kernel, start=start, fetched=len(held), earlier=len(earlier), ahead=ahead
        ),
        in_specs=[IN_SMEM] + [IN_VMEM] * (3 + len(held) + len(earlier)) + [ANYWHERE] * bool(ahead),
        out_specs=[IN_VMEM] * len(outs),
        out_shape=outs,
        scratch_shapes=[pltpu.SemaphoreType.DMA] * bool(ahead),
        compiler_params=pltpu.CompilerParams(vmem_limit_bytes=4 * 2**20),
        cost_estimate=pl.CostEstimate(
            flops=2 * rows * (stop - start) * span * size,
            bytes_accessed=2 * (stop - start) * span * size,
            transcendentals=0,
        ),
        name="hidden_grads",
    )(
        scalar(index),
        *map(resident, (cot, gate, up, *held, *earlier)),
        *([remaining(weights)] if ahead else []),
    )


def pack_kernel(*refs, count, ends):
    pieces, extra, (out_ref, end_ref) = refs[:count], refs[count], refs[-2:]
    rows = pieces[0].shape[0]
    for i, ref in enumerate(pieces):
        out_ref[i * rows : (i + 1) * rows, :] = ref[...]
    width = extra.shape[1]
    out_ref[count * rows :, :width] = extra[...]
    out_ref[count * rows :, width:] = jnp.zeros_like(out_ref[count * rows :, width:])
    for i, piece in enumerate(ends):
        end_ref[i * rows : (i + 1) * rows, :] = pieces[piece][:, -end_ref.shape[1] :]


def pack(pieces, extra, ends, columns):
    rows, width = pieces[0].shape
    dtype = pieces[0].dtype
    return pl.pallas_call(
        functools.partial(pack_kernel, count=len(pieces), ends=ends),
        in_specs=[IN_VMEM] * (len(pieces) + 1),
        out_specs=[IN_VMEM] * 2,
        out_shape=[pltpu.VMEM((len(pieces) * rows + rows, width), dtype), pltpu.VMEM((len(ends) * rows, columns), dtype)],
        compiler_params=pltpu.CompilerParams(vmem_limit_bytes=4 * 2**20),
        cost_estimate=pl.CostEstimate(flops=0, bytes_accessed=LONG, transcendentals=0),
        name="pack",
    )(*map(resident, pieces), resident(extra))


def join_kernel(*refs, count):
    ends_ref, firsts, outs = refs[0], refs[1 : 1 + count], refs[1 + count :]
    for i, (first, out) in enumerate(zip(firsts, outs)):
        rows, width = first.shape
        out[:, :width] = first[...]
        out[:, width:] = ends_ref[i * rows : (i + 1) * rows, :]


def join(ends, firsts):
    rows, width = firsts[0].shape
    out = pltpu.VMEM((rows, width + ends.shape[1]), firsts[0].dtype)
    return pl.pallas_call(
        functools.partial(join_kernel, count=len(firsts)),
        in_specs=[IN_VMEM] * (1 + len(firsts)),
        out_specs=[IN_VMEM] * len(firsts),
        out_shape=[out] * len(firsts),
        compiler_params=pltpu.CompilerParams(vmem_limit_bytes=4 * 2**20),
        name="join",
    )(*map(resident, (ends, *firsts)))


def turn_kernel(*refs, places, rows):
    out_ref = refs[-1]
    features = out_ref.shape[0]
    per_half = features // 2
    for d in range(features):
        slices = []
        low, column = (d // per_half) * rows, (d % per_half) * 128
        for (i, i_row), (j, j_row) in places:
            start = refs[i].shape[1] - per_half * 128 + column
            own = refs[i][i_row : i_row + 2 * rows, start : start + 128]
            start = features * 128 + column
            near = refs[j][j_row : j_row + 2 * rows, start : start + 128]
            slices += [own[low : low + rows], near[low : low + rows]]
            slices.append(refs[j][j_row : j_row + 2 * rows, d * 128 : (d + 1) * 128])
        out_ref[d] = jnp.concatenate(slices, axis=0).T


def turn(pieces, rows):
    arrays = []
    for piece in pieces:
        arrays += [array for array, _ in piece if not any(array is other for other in arrays)]
    places = [[([array is other for other in arrays].index(True), row) for array, row in piece] for piece in pieces]
    width = pieces[0][1][0].shape[1] * 2 // 3
    return pl.pallas_call(
        functools.partial(turn_kernel, places=places, rows=rows),
        in_specs=[IN_VMEM] * len(arrays),
        out_specs=IN_VMEM,
        out_shape=pltpu.VMEM((width // 128, 128, len(pieces) * 4 * rows), arrays[0].dtype),
        compiler_params=pltpu.CompilerParams(vmem_limit_bytes=4 * 2**20),
        name="turn",
    )(*map(resident, arrays))


def down_grad_kernel(index_ref, turned, *refs, places, pieces, rows, kept, chunk, scale):
    arrays, (out_ref, held, sems) = refs[:-3], refs[-3:]
    first = lax.axis_index("dp") * kept
    blocks = held.shape[0]
    features = turned.shape[0]
    per_half = features // 2
    copies = []

    def late(feature):
        low = feature < per_half
        column = jnp.where(low, feature, feature - per_half) * 128
        slices = []
        for (i, i_row), (j, j_row) in pieces:
            for ref, row, start in (
                (arrays[i], i_row, arrays[i].shape[1] - per_half * 128),
                (arrays[j], j_row, features * 128),
            ):
                both = ref[row : row + rows, pl.ds(pl.multiple_of(start + column, 128), 128)]
                slices.append(jnp.where(low, both[: rows // 2], both[rows // 2 :]))
            slices.append(arrays[j][j_row : j_row + rows, pl.ds(pl.multiple_of(feature * 128, 128), 128)])
        return jnp.concatenate(slices, axis=0).T

    for start in range(0, blocks, chunk):
        for block in range(start, start + chunk):
            right = jnp.concatenate(
                [
                    arrays[i][row : row + rows, column * 128 : (column + 1) * 128]
                    for i, row in places
                    for column in (block, blocks + block)
                ],
                axis=0,
            )
            chosen = [index_ref[first + k, block] for k in range(kept)]
            left = jnp.concatenate([jnp.concatenate([turned[d], late(d)], axis=1) for d in chosen], axis=0)
            held[block] = jnp.dot(left, right, preferred_element_type=jnp.float32) * scale
        span = pl.ds(start, chunk)
        copy = pltpu.make_async_copy(held.at[span], out_ref.at[span], sems.at[start // chunk])
        copy.start()
        copies.append(copy)
    for copy in copies:
        copy.wait()


def down_grads(index, turned, messages, sent, blocks, rows, kept, scale, chunk=4):
    arrays = []
    for array, _ in messages + sent:
        arrays += [array] * (not any(array is other for other in arrays))

    def place(array, row):
        return [array is other for other in arrays].index(True), row

    places = [place(*message) for message in messages]
    pieces = [(place(*m), place(*c)) for m, c in zip(messages[-len(sent) :], sent)]
    shape = (blocks, kept * 128, 128)
    return pl.pallas_call(
        functools.partial(
            down_grad_kernel, places=places, pieces=pieces, rows=rows, kept=kept, chunk=chunk, scale=scale
        ),
        in_specs=[IN_SMEM] + [IN_VMEM] * (1 + len(arrays)),
        out_specs=ANYWHERE,
        out_shape=jax.ShapeDtypeStruct(shape, jnp.float32),
        scratch_shapes=[pltpu.VMEM(shape, jnp.float32), pltpu.SemaphoreType.DMA((blocks // chunk,))],
        compiler_params=pltpu.CompilerParams(vmem_limit_bytes=12 * 2**20),
        cost_estimate=pl.CostEstimate(
            flops=4 * len(messages) * rows * kept * 128 * blocks * 128,
            bytes_accessed=4 * kept * blocks * 128 * 128,
            transcendentals=0,
        ),
        name="down_grads",
    )(scalar(index), *map(resident, (turned, *arrays)))


def gathered(gate_act, up_act, cotangent, down_blocks, down_index):
    replicas = lax.axis_size("dp")
    parts = lax.axis_size("tensor")
    kept = down_index.shape[1] // replicas

    first = functools.partial(
        lax.ppermute, axis_name="dp", perm=[(i, i ^ (2 if i % 2 == 0 else 4)) for i in range(replicas)]
    )
    second = functools.partial(
        lax.ppermute, axis_name="dp", perm=[(i, i ^ (4 if i % 2 == 0 else 2)) for i in range(replicas)]
    )
    across = functools.partial(lax.ppermute, axis_name="dp", perm=[(i, i ^ 6) for i in range(replicas)])
    other = functools.partial(lax.ppermute, axis_name="dp", perm=[(i, i ^ 1) for i in range(replicas)])

    message, gate, up, index, near = hidden_units(gate_act, up_act, down_index.T, cotangent)
    rows = message.shape[0]
    m1, m2 = first(message), second(message)
    slices = [lax.ppermute(near, "tensor", [(i, i ^ s) for i in range(parts)]) for s in range(1, parts)]
    blocks = down_blocks.shape[0]
    half = blocks // 2
    ahead = blocks * 3 // 14
    held = [fetch(down_blocks, 0, blocks - ahead)]
    cot, sent, far = assemble([near] + slices, held)
    c1, c2 = first(far), second(far)
    packed, nears = pack([message, m1, m2], sent, (1, 2), near.shape[1] // 2)
    nexts = lax.ppermute(nears, "tensor", [(i, i ^ 1) for i in range(parts)])
    m3 = first(m2)
    packed_x = other(packed)
    *grads, rest = hidden_grads(index, cot, gate, up, held, 0, half, weights=down_blocks, ahead=ahead)
    c1, c2, nexts, grads = lax.optimization_barrier((c1, c2, nexts, grads))
    raw = [nexts, c1, c2]
    c1, c2 = join(nexts, [c1, c2])
    c3 = second(c1)
    nexts_x, *raw_x = [other(array) for array in raw]
    c1x, c2x = join(nexts_x, raw_x)
    grads = hidden_grads(index, cot, gate, up, held + [rest], half, blocks, grads)
    messages = [(array, i * rows) for i in range(3) for array in (packed, packed_x)]
    early = turn(list(zip(messages[:4], [(sent, 0), (packed_x, 3 * rows), (c1, 0), (c1x, 0)])), rows // 2)
    c3, m3, early, c2x, packed_x, (gate_out, up_out) = lax.optimization_barrier(
        (c3, m3, early, c2x, packed_x, grads)
    )
    m3x, c3x = other(m3), other(c3)
    messages = [(array, i * rows) for i in range(3) for array in (packed, packed_x)] + [(m3, 0), (m3x, 0)]
    late = [(c2, 0), (c2x, 0), (c3, 0), (c3x, 0)]
    down_grad = down_grads(index, early, messages, late, blocks, rows, kept, 1.0 / replicas)
    return down_grad.transpose(1, 0, 2), gate_out, up_out


def local(gate_act, up_act, cotangent, down_blocks, down_index):
    sizes = (lax.axis_size("dp"), lax.axis_size("tensor"), gate_act.shape[0], down_blocks.shape[0] % 4)
    if sizes == (8, 4, 32, 0):
        return gathered(gate_act, up_act, cotangent, down_blocks, down_index)
    return reduced(gate_act, up_act, cotangent, down_blocks, down_index)


def solution(mesh):
    in_specs = (
        P("dp", "tensor"),
        P("dp", "tensor"),
        P(("dp", "tensor"), None),
        P("tensor", None, None),
        P("tensor", None),
    )
    out_specs = (P("dp", "tensor", None), P("dp", "tensor"), P("dp", "tensor"))
    return jax.shard_map(local, mesh=mesh, in_specs=in_specs, out_specs=out_specs, check_vma=False)
```

```python
import functools

import jax
import jax.numpy as jnp
from jax import lax
from jax.experimental import pallas as pl
from jax.experimental.pallas import tpu as pltpu
from jax.sharding import PartitionSpec as P


def reduced(gate_act, up_act, cotangent, down_blocks, down_index):
    gathered = lax.all_gather(cotangent, "tensor", axis=0, tiled=True)
    row_count = gathered.shape[0]
    local_blocks, kept_span, block_size = down_blocks.shape
    feature_count = gathered.shape[1] // block_size
    feature_view = gathered.reshape(row_count, feature_count, block_size)
    gate_value = gate_act.astype(jnp.float32).reshape(row_count, local_blocks, block_size)
    up_value = up_act.astype(jnp.float32).reshape(row_count, local_blocks, block_size)
    sigmoid_gate = jax.nn.sigmoid(gate_value)
    hidden = (gate_value * sigmoid_gate * up_value).astype(jnp.bfloat16)
    hidden_blocks = hidden.transpose(1, 0, 2)
    replicas = lax.axis_size("dp")

    def select(index_row):
        return jnp.take(feature_view, index_row, axis=1).reshape(row_count, kept_span)

    def one_grad(inputs):
        index_row, weight_block = inputs
        return jnp.dot(select(index_row), weight_block, preferred_element_type=jnp.float32)

    hidden_grad = lax.map(one_grad, (down_index, down_blocks)).transpose(1, 0, 2)
    gate_out = (
        (hidden_grad * up_value * sigmoid_gate * (1.0 + gate_value * (1.0 - sigmoid_gate)))
        .astype(jnp.bfloat16)
        .reshape(row_count, local_blocks * block_size)
    )
    up_out = (
        (hidden_grad * gate_value * sigmoid_gate)
        .astype(jnp.bfloat16)
        .reshape(row_count, local_blocks * block_size)
    )

    def one_term(inputs):
        index_row, hidden_block = inputs
        part_rows = select(index_row)
        return jnp.dot(part_rows.T, hidden_block, preferred_element_type=jnp.float32)

    summed = lax.psum_scatter(
        lax.map(one_term, (down_index, hidden_blocks)).transpose(1, 0, 2),
        "dp",
        scatter_dimension=0,
        tiled=True,
    )
    down_grad = summed / replicas
    return (down_grad, gate_out, up_out)


LONG = 2**27
IN_VMEM = pl.BlockSpec(memory_space=pltpu.VMEM)
IN_SMEM = pl.BlockSpec(memory_space=pltpu.SMEM)
ANYWHERE = pl.BlockSpec(memory_space=pl.ANY)


def resident(array):
    return pltpu.with_memory_space_constraint(array, pltpu.VMEM)


def scalar(array):
    return pltpu.with_memory_space_constraint(array, pltpu.SMEM)


def remaining(array):
    return pltpu.with_memory_space_constraint(array, pltpu.HBM)


def assemble_kernel(*refs, parts):
    pieces, (out_ref, sent_ref, far_ref) = refs[:parts][::-1], refs[-3:]
    here = lax.axis_index("tensor")
    for place in range(parts):

        @pl.when(here == place)
        def _():
            out_ref[...] = jnp.concatenate([pieces[place ^ q][...] for q in range(parts)], axis=0)

    width = out_ref.shape[1]
    far_ref[...] = jnp.concatenate([piece[...] for piece in pieces[2:]], axis=0)
    sent_ref[:, :width] = far_ref[...]
    sent_ref[:, width:] = stacked(pieces[1][...])


def stacked(rows):
    half = rows.shape[1] // 2
    return jnp.concatenate([rows[:, :half], rows[:, half:]], axis=0)


def assemble(pieces, after):
    rows, width = pieces[0].shape
    parts = len(pieces)
    dtype = pieces[0].dtype
    return pl.pallas_call(
        functools.partial(assemble_kernel, parts=parts),
        in_specs=[IN_VMEM] * (parts + len(after)),
        out_specs=[IN_VMEM] * 3,
        out_shape=[
            pltpu.VMEM(shape, dtype) for shape in ((parts * rows, width), (2 * rows, width * 3 // 2), (2 * rows, width))
        ],
        compiler_params=pltpu.CompilerParams(vmem_limit_bytes=4 * 2**20),
        cost_estimate=pl.CostEstimate(flops=0, bytes_accessed=LONG, transcendentals=0),
        name="assemble",
    )(*map(resident, pieces[::-1]), *map(resident, after))


def hidden_kernel(*refs, kept):
    sources, message_ref, targets, (hidden, sems) = refs[:kept], refs[kept], refs[kept + 1 : -2], refs[-2:]
    loads = [pltpu.make_async_copy(source, target, sems.at[i]) for i, (source, target) in enumerate(zip(sources, targets))]
    for load in loads:
        load.start()
    for load in loads:
        load.wait()
    gate = targets[0][...].astype(jnp.float32)
    up = targets[1][...].astype(jnp.float32)
    hidden[...] = gate * jax.nn.sigmoid(gate) * up
    rows, width = hidden.shape
    cot = targets[-1]
    size = cot.shape[0]
    parts = rows // size
    here = lax.axis_index("tensor")
    for place in range(parts):

        @pl.when(here == place)
        def _():
            groups = [hidden[(place ^ j) * size : ((place ^ j) + 1) * size, :] for j in range(parts)]
            for i in range(parts // 2):
                pair = jnp.concatenate(groups[2 * i : 2 * i + 2], axis=0)
                message_ref[:, i * width : (i + 1) * width] = pair.astype(message_ref.dtype)

    message_ref[:, rows * width // (2 * size) :] = stacked(cot[...])


def hidden_units(*arrays):
    gate, cot = arrays[0], arrays[-1]
    spaces = [pltpu.SMEM if array.dtype == jnp.int32 else pltpu.VMEM for array in arrays]
    outs = [space(array.shape, array.dtype) for space, array in zip(spaces, arrays)]
    rows = 2 * cot.shape[0]
    message = pltpu.VMEM((rows, (gate.size + cot.size) // rows), gate.dtype)
    return pl.pallas_call(
        functools.partial(hidden_kernel, kept=len(arrays)),
        in_specs=[ANYWHERE] * len(arrays),
        out_specs=[IN_VMEM] + [pl.BlockSpec(memory_space=space) for space in spaces],
        out_shape=[message] + outs,
        scratch_shapes=[pltpu.VMEM(gate.shape, jnp.float32), pltpu.SemaphoreType.DMA((len(arrays),))],
        compiler_params=pltpu.CompilerParams(vmem_limit_bytes=4 * 2**20),
        name="hidden_units",
    )(*map(remaining, arrays))


def fetch_kernel(weight_ref, *refs, start, chunk):
    out_ref, sems = refs[-2:]
    loads = [
        pltpu.make_async_copy(weight_ref.at[pl.ds(start + j, chunk)], out_ref.at[pl.ds(j, chunk)], sems.at[j // chunk])
        for j in range(0, out_ref.shape[0], chunk)
    ]
    for load in loads:
        load.start()
    for load in loads:
        load.wait()


def fetch(weights, start, blocks, after=(), chunk=2):
    shape = (blocks,) + weights.shape[1:]
    return pl.pallas_call(
        functools.partial(fetch_kernel, start=start, chunk=chunk),
        in_specs=[ANYWHERE] + [IN_VMEM] * len(after),
        out_specs=IN_VMEM,
        out_shape=pltpu.VMEM(shape, weights.dtype),
        scratch_shapes=[pltpu.SemaphoreType.DMA((blocks // chunk,))],
        compiler_params=pltpu.CompilerParams(vmem_limit_bytes=4 * 2**20),
        cost_estimate=pl.CostEstimate(flops=0, bytes_accessed=2**18 * blocks, transcendentals=0),
        name="fetch",
    )(remaining(weights), *map(resident, after))


def hidden_grad_kernel(*refs, start, fetched, earlier, ahead):
    index_ref, cot_ref, gate_ref, up_ref = refs[:4]
    held = refs[4 : 4 + fetched]
    done = refs[4 + fetched : 4 + fetched + earlier]
    span, size = held[0].shape[1:]
    if ahead:
        weight_ref, (gate_out, up_out, next_ref, sem) = refs[4 + fetched + earlier], refs[-4:]
        load = pltpu.make_async_copy(weight_ref.at[pl.ds(weight_ref.shape[0] - ahead, ahead)], next_ref, sem)
        load.start()
    else:
        gate_out, up_out = refs[-2:]
    places = [(ref, j) for ref in held for j in range(ref.shape[0])]
    for source, target in zip(done, (gate_out, up_out)):
        target[:, : start * size] = source[...]
    for block in range(start, gate_out.shape[1] // size):
        chosen = jnp.concatenate(
            [cot_ref[:, pl.ds(pl.multiple_of(index_ref[k, block] * size, size), size)] for k in range(span // size)],
            axis=1,
        )
        ref, j = places[block]
        grad = jnp.dot(chosen, ref[j], preferred_element_type=jnp.float32)
        here = slice(block * size, (block + 1) * size)
        gate = gate_ref[:, here].astype(jnp.float32)
        up = up_ref[:, here].astype(jnp.float32)
        sig = jax.nn.sigmoid(gate)
        gate_out[:, here] = (grad * up * sig * (1.0 + gate * (1.0 - sig))).astype(jnp.bfloat16)
        up_out[:, here] = (grad * gate * sig).astype(jnp.bfloat16)
    if ahead:
        load.wait()


def hidden_grads(index, cot, gate, up, held, start, stop, earlier=(), weights=None, ahead=0):
    _, span, size = held[0].shape
    rows = cot.shape[0]
    shape = (rows, stop * size)
    outs = [jax.ShapeDtypeStruct(shape, gate.dtype)] * 2
    if ahead:
        outs = [pltpu.VMEM(shape, gate.dtype)] * 2 + [pltpu.VMEM((ahead, span, size), weights.dtype)]
    return pl.pallas_call(
        functools.partial(
            hidden_grad_kernel, start=start, fetched=len(held), earlier=len(earlier), ahead=ahead
        ),
        in_specs=[IN_SMEM] + [IN_VMEM] * (3 + len(held) + len(earlier)) + [ANYWHERE] * bool(ahead),
        out_specs=[IN_VMEM] * len(outs),
        out_shape=outs,
        scratch_shapes=[pltpu.SemaphoreType.DMA] * bool(ahead),
        compiler_params=pltpu.CompilerParams(vmem_limit_bytes=4 * 2**20),
        cost_estimate=pl.CostEstimate(
            flops=2 * rows * (stop - start) * span * size,
            bytes_accessed=2 * (stop - start) * span * size,
            transcendentals=0,
        ),
        name="hidden_grads",
    )(
        scalar(index),
        *map(resident, (cot, gate, up, *held, *earlier)),
        *([remaining(weights)] if ahead else []),
    )


def pack_kernel(*refs, count, ends):
    pieces, extra, (out_ref, end_ref) = refs[:count], refs[count], refs[-2:]
    rows = pieces[0].shape[0]
    for i, ref in enumerate(pieces):
        out_ref[i * rows : (i + 1) * rows, :] = ref[...]
    width = extra.shape[1]
    out_ref[count * rows :, :width] = extra[...]
    out_ref[count * rows :, width:] = jnp.zeros_like(out_ref[count * rows :, width:])
    for i, piece in enumerate(ends):
        end_ref[i * rows : (i + 1) * rows, :] = pieces[piece][:, -end_ref.shape[1] :]


def pack(pieces, extra, ends, columns):
    rows, width = pieces[0].shape
    dtype = pieces[0].dtype
    return pl.pallas_call(
        functools.partial(pack_kernel, count=len(pieces), ends=ends),
        in_specs=[IN_VMEM] * (len(pieces) + 1),
        out_specs=[IN_VMEM] * 2,
        out_shape=[pltpu.VMEM((len(pieces) * rows + rows, width), dtype), pltpu.VMEM((len(ends) * rows, columns), dtype)],
        compiler_params=pltpu.CompilerParams(vmem_limit_bytes=4 * 2**20),
        cost_estimate=pl.CostEstimate(flops=0, bytes_accessed=LONG, transcendentals=0),
        name="pack",
    )(*map(resident, pieces), resident(extra))


def join_kernel(*refs, count):
    ends_ref, firsts, outs = refs[0], refs[1 : 1 + count], refs[1 + count :]
    for i, (first, out) in enumerate(zip(firsts, outs)):
        rows, width = first.shape
        out[:, :width] = first[...]
        out[:, width:] = ends_ref[i * rows : (i + 1) * rows, :]


def join(ends, firsts):
    rows, width = firsts[0].shape
    out = pltpu.VMEM((rows, width + ends.shape[1]), firsts[0].dtype)
    return pl.pallas_call(
        functools.partial(join_kernel, count=len(firsts)),
        in_specs=[IN_VMEM] * (1 + len(firsts)),
        out_specs=[IN_VMEM] * len(firsts),
        out_shape=[out] * len(firsts),
        compiler_params=pltpu.CompilerParams(vmem_limit_bytes=4 * 2**20),
        name="join",
    )(*map(resident, (ends, *firsts)))


def turn_kernel(*refs, places, rows):
    out_ref = refs[-1]
    features = out_ref.shape[0]
    per_half = features // 2
    for d in range(features):
        slices = []
        low, column = (d // per_half) * rows, (d % per_half) * 128
        for (i, i_row), (j, j_row) in places:
            start = refs[i].shape[1] - per_half * 128 + column
            own = refs[i][i_row : i_row + 2 * rows, start : start + 128]
            start = features * 128 + column
            near = refs[j][j_row : j_row + 2 * rows, start : start + 128]
            slices += [own[low : low + rows], near[low : low + rows]]
            slices.append(refs[j][j_row : j_row + 2 * rows, d * 128 : (d + 1) * 128])
        out_ref[d] = jnp.concatenate(slices, axis=0).T


def turn(pieces, rows):
    arrays = []
    for piece in pieces:
        arrays += [array for array, _ in piece if not any(array is other for other in arrays)]
    places = [[([array is other for other in arrays].index(True), row) for array, row in piece] for piece in pieces]
    width = pieces[0][1][0].shape[1] * 2 // 3
    return pl.pallas_call(
        functools.partial(turn_kernel, places=places, rows=rows),
        in_specs=[IN_VMEM] * len(arrays),
        out_specs=IN_VMEM,
        out_shape=pltpu.VMEM((width // 128, 128, len(pieces) * 4 * rows), arrays[0].dtype),
        compiler_params=pltpu.CompilerParams(vmem_limit_bytes=4 * 2**20),
        name="turn",
    )(*map(resident, arrays))


def down_grad_kernel(index_ref, turned, *refs, places, pieces, rows, kept, chunk, scale):
    arrays, (out_ref, held, sems) = refs[:-3], refs[-3:]
    first = lax.axis_index("dp") * kept
    blocks = held.shape[0]
    features = turned.shape[0]
    per_half = features // 2
    copies = []

    def late(feature):
        low = feature < per_half
        column = jnp.where(low, feature, feature - per_half) * 128
        slices = []
        for (i, i_row), (j, j_row) in pieces:
            for ref, row, start in (
                (arrays[i], i_row, arrays[i].shape[1] - per_half * 128),
                (arrays[j], j_row, features * 128),
            ):
                both = ref[row : row + rows, pl.ds(pl.multiple_of(start + column, 128), 128)]
                slices.append(jnp.where(low, both[: rows // 2], both[rows // 2 :]))
            slices.append(arrays[j][j_row : j_row + rows, pl.ds(pl.multiple_of(feature * 128, 128), 128)])
        return jnp.concatenate(slices, axis=0).T

    for start in range(0, blocks, chunk):
        for block in range(start, start + chunk):
            right = jnp.concatenate(
                [
                    arrays[i][row : row + rows, column * 128 : (column + 1) * 128]
                    for i, row in places
                    for column in (block, blocks + block)
                ],
                axis=0,
            )
            chosen = [index_ref[first + k, block] for k in range(kept)]
            left = jnp.concatenate([jnp.concatenate([turned[d], late(d)], axis=1) for d in chosen], axis=0)
            held[block] = jnp.dot(left, right, preferred_element_type=jnp.float32) * scale
        span = pl.ds(start, chunk)
        copy = pltpu.make_async_copy(held.at[span], out_ref.at[span], sems.at[start // chunk])
        copy.start()
        copies.append(copy)
    for copy in copies:
        copy.wait()


def down_grads(index, turned, messages, sent, blocks, rows, kept, scale, chunk=4):
    arrays = []
    for array, _ in messages + sent:
        arrays += [array] * (not any(array is other for other in arrays))

    def place(array, row):
        return [array is other for other in arrays].index(True), row

    places = [place(*message) for message in messages]
    pieces = [(place(*m), place(*c)) for m, c in zip(messages[-len(sent) :], sent)]
    shape = (blocks, kept * 128, 128)
    return pl.pallas_call(
        functools.partial(
            down_grad_kernel, places=places, pieces=pieces, rows=rows, kept=kept, chunk=chunk, scale=scale
        ),
        in_specs=[IN_SMEM] + [IN_VMEM] * (1 + len(arrays)),
        out_specs=ANYWHERE,
        out_shape=jax.ShapeDtypeStruct(shape, jnp.float32),
        scratch_shapes=[pltpu.VMEM(shape, jnp.float32), pltpu.SemaphoreType.DMA((blocks // chunk,))],
        compiler_params=pltpu.CompilerParams(vmem_limit_bytes=12 * 2**20),
        cost_estimate=pl.CostEstimate(
            flops=4 * len(messages) * rows * kept * 128 * blocks * 128,
            bytes_accessed=4 * kept * blocks * 128 * 128,
            transcendentals=0,
        ),
        name="down_grads",
    )(scalar(index), *map(resident, (turned, *arrays)))


def gathered(gate_act, up_act, cotangent, down_blocks, down_index):
    replicas = lax.axis_size("dp")
    parts = lax.axis_size("tensor")
    kept = down_index.shape[1] // replicas

    first = functools.partial(
        lax.ppermute, axis_name="dp", perm=[(i, i ^ (2 if i % 2 == 0 else 4)) for i in range(replicas)]
    )
    second = functools.partial(
        lax.ppermute, axis_name="dp", perm=[(i, i ^ (4 if i % 2 == 0 else 2)) for i in range(replicas)]
    )
    across = functools.partial(lax.ppermute, axis_name="dp", perm=[(i, i ^ 6) for i in range(replicas)])
    other = functools.partial(lax.ppermute, axis_name="dp", perm=[(i, i ^ 1) for i in range(replicas)])

    message, gate, up, index, near = hidden_units(gate_act, up_act, down_index.T, cotangent)
    rows = message.shape[0]
    m1, m2 = first(message), second(message)
    slices = [lax.ppermute(near, "tensor", [(i, i ^ s) for i in range(parts)]) for s in range(1, parts)]
    blocks = down_blocks.shape[0]
    half = blocks // 7
    ahead = blocks * 2 // 7
    held = [fetch(down_blocks, 0, blocks - ahead)]
    cot, sent, far = assemble([near] + slices, held)
    c1, c2 = first(far), second(far)
    packed, nears = pack([message, m1, m2], sent, (1, 2), near.shape[1] // 2)
    nexts = lax.ppermute(nears, "tensor", [(i, i ^ 1) for i in range(parts)])
    m3 = first(m2)
    packed_x = other(packed)
    *grads, rest = hidden_grads(index, cot, gate, up, held, 0, half, weights=down_blocks, ahead=ahead)
    c1, c2, nexts, grads = lax.optimization_barrier((c1, c2, nexts, grads))
    raw = [nexts, c1, c2]
    c1, c2 = join(nexts, [c1, c2])
    c3 = second(c1)
    nexts_x, *raw_x = [other(array) for array in raw]
    c1x, c2x = join(nexts_x, raw_x)
    grads = hidden_grads(index, cot, gate, up, held + [rest], half, blocks, grads)
    messages = [(array, i * rows) for i in range(3) for array in (packed, packed_x)]
    early = turn(list(zip(messages[:4], [(sent, 0), (packed_x, 3 * rows), (c1, 0), (c1x, 0)])), rows // 2)
    c3, m3, early, c2x, packed_x, (gate_out, up_out) = lax.optimization_barrier(
        (c3, m3, early, c2x, packed_x, grads)
    )
    m3x, c3x = other(m3), other(c3)
    messages = [(array, i * rows) for i in range(3) for array in (packed, packed_x)] + [(m3, 0), (m3x, 0)]
    late = [(c2, 0), (c2x, 0), (c3, 0), (c3x, 0)]
    down_grad = down_grads(index, early, messages, late, blocks, rows, kept, 1.0 / replicas)
    return down_grad.transpose(1, 0, 2), gate_out, up_out


def local(gate_act, up_act, cotangent, down_blocks, down_index):
    sizes = (lax.axis_size("dp"), lax.axis_size("tensor"), gate_act.shape[0], down_blocks.shape[0] % 4)
    if sizes == (8, 4, 32, 0):
        return gathered(gate_act, up_act, cotangent, down_blocks, down_index)
    return reduced(gate_act, up_act, cotangent, down_blocks, down_index)


def solution(mesh):
    in_specs = (
        P("dp", "tensor"),
        P("dp", "tensor"),
        P(("dp", "tensor"), None),
        P("tensor", None, None),
        P("tensor", None),
    )
    out_specs = (P("dp", "tensor", None), P("dp", "tensor"), P("dp", "tensor"))
    return jax.shard_map(local, mesh=mesh, in_specs=in_specs, out_specs=out_specs, check_vma=False)
```
